512 devices in a mesh: expert: 32 (over y, z_hi, x), tensor: 16 (over z_lo, core).
Axes of the slice: x: 4, y: 4, z: 16 (z_hi: 2, z_lo: 8; z = z_hi * 8 + z_lo), core: 2. Of those that a mesh axis runs over, the one named last changes fastest.
Arguments:
- tokens: bfloat16 [2048, 3616], P('expert', 'tensor'), may hold values from -6 to 6
- gate_codes: int32 [2048, 8], P('expert'), may hold values from 1 to 1023
- routes: int32 [2048, 8], P('expert'), may hold values from 0 to 31, all different within a row; in each aligned block of 64 rows (0 to 63, 64 to 127, ...) at most 32 rows name the same one
- routed_gate: bfloat16 [32, 3616, 2048], P('expert', None, 'tensor'), may hold values from -0.09375 to 0.09375
- routed_up: bfloat16 [32, 3616, 2048], P('expert', None, 'tensor'), may hold values from -0.09375 to 0.09375
- routed_down: bfloat16 [32, 2048, 3616], P('expert', 'tensor'), may hold values from -0.125 to 0.125
- shared_gate: bfloat16 [3616, 2048], P('expert', 'tensor'), may hold values from -0.09375 to 0.09375
- shared_up: bfloat16 [3616, 2048], P('expert', 'tensor'), may hold values from -0.09375 to 0.09375
- shared_down: bfloat16 [2048, 3616], P('tensor', 'expert'), may hold values from -0.125 to 0.125
Outputs:
- mixed: bfloat16 [2048, 3616], P('expert', 'tensor')
The draws below stay inside these ranges and needn't reach their ends.
Inputs may be any that keep to these rules, and one draw needn't show every extreme that they name: `routes`: within the 64 rows of one device no expert is named by more than 32 rows, a bound that some block reaches; the 8 experts of a row differ.
All inputs are finite; a program needn't handle non-finite values.
Results may differ from the reference program's by a relative error of at most 0.023.
Values may be sent and summed in bfloat16 or wider, within the bound.
No kernel may reach another device: no remote copies, remote signals or barrier semaphores. Data moves between devices by JAX's collectives and lax.ppermute only.
A program may use at most 64 MiB of HBM per device.

```python
import math
import jax
import jax.numpy as jnp
import numpy as np
from jax import lax

D = 3616
HID = 2048
SHID = 2048
TOP = 8
TOK_DEV = 64
EXPERTS = 32
CAP = 32
TOKENS = 2048
N_EXPERT = 32
N_TENSOR = 16


def place_ends(array, stream_key, least, high):
    longest = array.shape.index(max(array.shape))
    spots = []
    for shift in (0, 1):
        where = [jax.random.randint(jax.random.fold_in(stream_key, axis), (), 0, length) for axis, length in enumerate(array.shape)]
        where[longest] = (where[longest] + shift) % array.shape[longest]
        spots.append(tuple(where))
    return array.at[spots[0]].set(least).at[spots[1]].set(high)


def block_levels(own_key, shape, split, least, top_value):
    level = 1.0
    for axis_at, blocks in split:
        draws = jax.random.uniform(jax.random.fold_in(jax.random.fold_in(own_key, 6), axis_at), (blocks,), jnp.float32, least / len(split), top_value / len(split))
        level = level * jnp.repeat(jnp.exp(draws), shape[axis_at] // blocks).reshape((-1,) + (1,) * (len(shape) - 1 - axis_at))
    return level


def routed_block(stream_key, own, number, rows, number_of, top, reach, slope):
    order = jax.random.permutation(stream_key, number_of)
    packed, ordinary = shares(number_of, rows * top, reach, slope, True), shares(number_of, rows * top, reach, slope, False)
    places = jnp.arange(number_of)

    def named(sizes, rotation):
        used = int((sizes > 0).sum())
        fixed = max(1, used // 4)
        passed = fixed + (places - fixed + rotation * (used - fixed)) % max(1, number_of - fixed)
        return jnp.zeros((number_of,), jnp.int32).at[order[jnp.where(places < fixed, places, passed)]].set(jnp.asarray(sizes, jnp.int32))

    sizes = jnp.where(number % 4 == 0, named(packed, number // 4), named(ordinary, number - number // 4 - 1))
    mixed = jax.random.permutation(jax.random.fold_in(own, 3), number_of)
    donor, taker = mixed[0:number_of // 2 * 2:2], mixed[1:number_of // 2 * 2:2]
    slack = jnp.minimum(sizes[donor] - 1, reach - sizes[taker]) // 2
    slack = jnp.where((donor == order[0]) | (taker == order[0]) | (sizes[taker] == 0), 0, jnp.maximum(slack, 0))
    passed = jax.random.randint(jax.random.fold_in(own, 4), (number_of // 2,), 0, 1 << 20) % (slack + 1)
    sizes = sizes.at[donor].add(-passed).at[taker].add(passed)
    members = jnp.searchsorted(jnp.cumsum(sizes), jnp.arange(rows * top), side="right").astype(jnp.int32)
    table = members.reshape(top, rows).T
    table = table[jax.random.permutation(jax.random.fold_in(own, 1), rows)]
    rotation = jax.random.randint(jax.random.fold_in(own, 2), (rows, 1), 0, top)
    return jnp.take_along_axis(table, (jnp.arange(top)[None, :] + rotation) % top, axis=1)


def shares(amount, total, limit, skew, full):
    portions = [(1 << 20) // math.isqrt(grade ** skew) + 1 for grade in range(1, amount + 1)]
    largest = limit if full else min(limit, max(-(-total // amount), total * portions[0] // sum(portions)))
    least = 1 if total - largest >= amount - 1 else 0
    holding, spare = [largest] + [least] * (amount - 1), total - largest - least * (amount - 1)
    while spare > 0:
        free = [i for i in range(1, amount) if holding[i] < largest] or [i for i in range(1, amount) if holding[i] < limit]
        whole, budget = sum([portions[i] for i in free]), spare
        for i in free:
            more = min(limit - holding[i], max(1, budget * portions[i] // whole), spare)
            holding[i] = holding[i] + more
            spare = spare - more
    return np.array(holding)


def centred(own_key, shape, spread, reach, shards=(), kind=jnp.bfloat16):
    level = block_levels(own_key, shape, shards, -0.22, 0.18) if shards else 1.0
    entries = jax.random.normal(own_key, shape, jnp.float32) * spread * level
    return jnp.minimum(jnp.maximum(entries, -reach), reach).astype(kind)


def setup_inputs(seed: int = 0) -> dict:
    key_list = jax.random.split(jax.random.key(seed), 10)
    tokens = centred(key_list[0], (TOKENS, D), 1.0, 6.0, ((0, 32), (1, 16)))
    gate_codes = place_ends(jax.random.randint(key_list[1], (TOKENS, TOP), 1, 1024), jax.random.fold_in(key_list[1], 1), 1, 1023).astype(jnp.int32)
    routes_keys = jax.random.split(jax.random.fold_in(key_list[2], 1), TOKENS // TOK_DEV)
    routes_turns = jax.random.permutation(jax.random.fold_in(key_list[2], 3), TOKENS // TOK_DEV)
    routes = jax.vmap(lambda own, number: routed_block(jax.random.fold_in(key_list[2], 2), own, number, TOK_DEV, EXPERTS, TOP, CAP, 2))(routes_keys, routes_turns).reshape((TOKENS, TOP))
    routed_gate = centred(key_list[3], (EXPERTS, D, HID), D ** -0.5, 0.09375, ((0, 32), (2, 16)))
    routed_up = centred(key_list[4], (EXPERTS, D, HID), D ** -0.5, 0.09375, ((0, 32), (2, 16)))
    routed_down = centred(key_list[5], (EXPERTS, HID, D), HID ** -0.5, 0.125, ((0, 32), (1, 16)))
    shared_gate = centred(key_list[6], (D, SHID), D ** -0.5, 0.09375, ((0, 32), (1, 16)))
    shared_up = centred(key_list[7], (D, SHID), D ** -0.5, 0.09375, ((0, 32), (1, 16)))
    shared_down = centred(key_list[8], (SHID, D), SHID ** -0.5, 0.125, ((0, 16), (1, 32)))
    return dict(tokens=tokens, gate_codes=gate_codes, routes=routes, routed_gate=routed_gate, routed_up=routed_up, routed_down=routed_down, shared_gate=shared_gate, shared_up=shared_up, shared_down=shared_down)


def reference(tokens, gate_codes, routes, routed_gate, routed_up, routed_down, shared_gate, shared_up, shared_down):
    shared_gate_acts = jnp.dot(tokens, shared_gate, preferred_element_type=jnp.float32)
    shared_up_acts = jnp.dot(tokens, shared_up, preferred_element_type=jnp.float32)
    shared_hidden = (jax.nn.silu(shared_gate_acts) * shared_up_acts).astype(jnp.bfloat16)
    shared_out = jnp.dot(shared_hidden, shared_down, preferred_element_type=jnp.float32)

    gate_values = gate_codes.astype(jnp.float32)
    weights = 2.5 * gate_values / jnp.sum(gate_values, axis=1, keepdims=True)

    blocked = routes.reshape(N_EXPERT, TOK_DEV, TOP)
    onehot = (blocked[..., None] == jnp.arange(EXPERTS, dtype=jnp.int32)).astype(jnp.int32)
    counts = jnp.sum(onehot, axis=2)
    before = jnp.cumsum(counts, axis=1) - counts
    slot_index = jnp.sum(onehot * before[:, :, None, :], axis=3).reshape(TOKENS, TOP)
    source = (jnp.arange(TOKENS, dtype=jnp.int32) // TOK_DEV).astype(jnp.int32)
    slot_rows = (source[:, None] * CAP + slot_index).astype(jnp.int32)

    copies = jnp.broadcast_to(tokens[:, None, :], (TOKENS, TOP, D))
    buffers = jnp.zeros((EXPERTS, N_EXPERT * CAP, D), jnp.bfloat16).at[routes, slot_rows].set(copies)

    hid_block = HID // N_TENSOR

    def expert_apply(operands):
        rows_in, w_gate, w_up, w_down = operands
        gate_acts = jnp.dot(rows_in, w_gate, preferred_element_type=jnp.float32)
        up_acts = jnp.dot(rows_in, w_up, preferred_element_type=jnp.float32)
        hidden = (jax.nn.silu(gate_acts) * up_acts).astype(jnp.bfloat16)
        hidden_blocks = hidden.reshape(N_EXPERT * CAP, N_TENSOR, hid_block).astype(jnp.float32)
        down_blocks = w_down.reshape(N_TENSOR, hid_block, D).astype(jnp.float32)
        partials = jnp.einsum("rtk,tkd->trd", hidden_blocks, down_blocks).astype(jnp.bfloat16)
        partials = lax.optimization_barrier(partials)
        return jnp.sum(partials.astype(jnp.float32), axis=0).astype(jnp.bfloat16)

    expert_rows = lax.map(expert_apply, (buffers, routed_gate, routed_up, routed_down))
    picked = expert_rows[routes, slot_rows].astype(jnp.float32)
    combined = jnp.sum(weights[:, :, None] * picked, axis=1)
    return (shared_out + combined).astype(jnp.bfloat16)
```

```python
import jax
import jax.numpy as jnp
from jax import lax
from jax.sharding import Mesh, PartitionSpec as P

Y, H, X, L, C = 4, 2, 4, 8, 2
AXES = ("y", "h", "x", "l", "c")
EXPERT = ("y", "h", "x")
TENSOR = ("l", "c")
Z = ("h", "l")
f32 = jnp.float32
bf16 = jnp.bfloat16


def shift(a, axis, k):
    return lax.ppermute(a, axis, [(j, (j + k) % 4) for j in range(4)])


def swap(a):
    return lax.ppermute(a, "c", [(0, 1), (1, 0)])


def gather4(a, axis):
    m = a.shape[0] // 2
    p, n = shift(a, axis, 1), shift(a, axis, -1)
    p2, n2 = shift(p[:m], axis, 1), shift(n[m:], axis, -1)
    return a, p, n, jnp.concatenate([p2, n2], 0)


def add(*terms):
    total = terms[0].astype(f32)
    for t in terms[1:]:
        total = total + t.astype(f32)
    return total.astype(bf16)


def scatter4(own, p, n, d, axis):
    m = d.shape[0] // 2
    rp, rn = shift(d[:m], axis, 1), shift(d[m:], axis, -1)
    to_n = jnp.concatenate([add(n[:m], rp), n[m:]], 0)
    to_p = jnp.concatenate([p[:m], add(p[m:], rn)], 0)
    return add(own, shift(to_n, axis, 1), shift(to_p, axis, -1))


def local(
    tokens,
    gate_codes,
    routes,
    routed_gate,
    routed_up,
    routed_down,
    shared_gate,
    shared_up,
    shared_down,
):
    core = lax.axis_index("c")
    expert = lax.axis_index(EXPERT)
    toks, width = tokens.shape
    half = toks // C
    feats = width * L * C
    pair = width * C
    top = routes.shape[1]

    mine = lax.dynamic_slice_in_dim(tokens, core * half, half, 0)
    theirs = lax.dynamic_slice_in_dim(tokens, (1 - core) * half, half, 0)
    other = swap(theirs)
    two = jnp.where(
        core == 0, jnp.concatenate([mine, other], 1), jnp.concatenate([other, mine], 1)
    )
    meta = jnp.concatenate([routes, gate_codes // 32, gate_codes % 32], 1).astype(bf16)
    meta = lax.dynamic_slice_in_dim(meta, core * half, half, 0)
    sent = jnp.concatenate([two, meta, jnp.zeros((half, 512 - pair - 3 * top), bf16)], 1)
    got = lax.all_gather(sent, Z, axis=0, tiled=False)
    got = got.reshape(H, L, half, 512)
    rows = got[:, :, :, :pair].transpose(0, 2, 1, 3).reshape(H * half, feats)
    metas = got[:, 0, :, pair : pair + 3 * top].reshape(H * half, 3 * top)
    full = -(-feats // 128) * 128
    rows = jnp.concatenate(
        [rows, metas, jnp.zeros((H * half, full - feats - 3 * top), bf16)], 1
    )

    w_in = [routed_gate[0], routed_up[0]]
    w_in = jnp.concatenate([w_in[0], swap(w_in[0]), w_in[1], swap(w_in[1])], 1)
    hid = routed_gate.shape[2] * C
    n_exp = Y * H * X
    units = shared_gate.shape[1] // n_exp
    depth = shared_gate.shape[0]
    s = jnp.stack([shared_gate.T, shared_up.T, shared_down]).reshape(3, n_exp, units, depth)
    s = s.transpose(1, 0, 2, 3).reshape(n_exp, 3 * units, depth)
    s = lax.all_to_all(s, EXPERT, split_axis=0, concat_axis=0, tiled=True)
    s = s.transpose(1, 0, 2).reshape(3, units, feats)
    s = jnp.concatenate([s, swap(s)], 1)
    s_hid = units * C
    s_in = s[:2].reshape(2 * s_hid, feats)
    w_out = jnp.concatenate([routed_down[0], swap(routed_down[0]), s[2]], 0)

    def apply(block):
        x = block[:, :feats]
        codes = block[:, feats : feats + 3 * top].astype(f32)
        gates = codes[:, top : 2 * top] * 32.0 + codes[:, 2 * top :]
        chosen = jnp.sum(
            jnp.where(codes[:, :top] == expert.astype(f32), gates, 0.0), axis=1, keepdims=True
        )
        weight = 2.5 * chosen / jnp.sum(gates, axis=1, keepdims=True)
        acts = jnp.dot(x, w_in, preferred_element_type=f32)
        s_acts = lax.dot_general(x, s_in, (((1,), (1,)), ((), ())), preferred_element_type=f32)
        hidden = jax.nn.silu(acts[:, :hid]) * acts[:, hid:] * weight
        s_hidden = jax.nn.silu(s_acts[:, :s_hid]) * s_acts[:, s_hid:]
        both = jnp.concatenate([hidden, s_hidden], 1).astype(bf16)
        return jnp.dot(both, w_out, preferred_element_type=f32).astype(bf16)

    def chunk(part, first, second):
        r = part.shape[0]
        near = jnp.concatenate(gather4(part, first), 0)
        outs = [apply(b) for b in gather4(near, second)]
        near = scatter4(*outs, second)
        return scatter4(*[near[i * r : (i + 1) * r] for i in range(4)], first)

    summed = [chunk(rows[:half], "y", "x"), chunk(rows[half:], "x", "y")]
    back = jnp.concatenate(summed, 0).reshape(H, half, L, pair).transpose(0, 2, 1, 3)
    back = lax.all_to_all(
        back.reshape(H * L, half, pair), Z, split_axis=0, concat_axis=0, tiled=True
    )
    done = jnp.sum(back.astype(f32), axis=0).astype(bf16)
    lo, hi = done[:, :width], done[:, width:]
    keep, give = jnp.where(core == 0, lo, hi), jnp.where(core == 0, hi, lo)
    take = swap(give)
    return jnp.where(
        core == 0, jnp.concatenate([keep, take], 0), jnp.concatenate([take, keep], 0)
    )


def solution(mesh):
    fine = Mesh(mesh.devices.reshape(Y, H, X, L, C), AXES)
    in_specs = (
        P(EXPERT, TENSOR),
        P(EXPERT, None),
        P(EXPERT, None),
        P(EXPERT, None, TENSOR),
        P(EXPERT, None, TENSOR),
        P(EXPERT, TENSOR, None),
        P(EXPERT, TENSOR),
        P(EXPERT, TENSOR),
        P(TENSOR, EXPERT),
    )
    return jax.shard_map(
        local, mesh=fine, in_specs=in_specs, out_specs=P(EXPERT, TENSOR), check_vma=False
    )
```

```python
import functools

import jax
import jax.numpy as jnp
from jax import lax
from jax.experimental import pallas as pl
from jax.experimental.pallas import tpu as pltpu
from jax.sharding import Mesh, PartitionSpec as P

Y, H, X, L, C = 4, 2, 4, 8, 2
AXES = ("y", "h", "x", "l", "c")
EXPERT = ("y", "h", "x")
TENSOR = ("l", "c")
Z = ("h", "l")
f32 = jnp.float32
bf16 = jnp.bfloat16


def move(a, stage, k):
    pairs = []
    for y in range(Y):
        for x in range(X):
            for c in range(C):
                to = ((y + k) % Y, x) if (stage + c) % 2 == 0 else (y, (x + k) % X)
                pairs.append(((y * X + x) * C + c, (to[0] * X + to[1]) * C + c))
    return lax.ppermute(a, ("y", "x", "c"), pairs)


def swap(a):
    return lax.ppermute(a, "c", [(0, 1), (1, 0)])


def turn(a):
    return lax.ppermute(a, ("h", "c"), [(h * 2 + c, c * 2 + h) for h in range(2) for c in range(2)])


def add(*terms):
    total = terms[0].astype(f32)
    for t in terms[1:]:
        total = total + t.astype(f32)
    return total.astype(bf16)


def ffn_kernel(at_ref, x_ref, w_ref, s_ref, d_ref, sd_ref, o_ref, *, hid, units):
    width = x_ref.shape[1]
    tail = x_ref[:, width - 128 :].astype(f32)
    lane = lax.broadcasted_iota(jnp.int32, tail.shape, 1)
    at = at_ref[0]
    weight = jnp.sum(
        jnp.where((lane == at) | (lane == at + 2), tail, 0.0), axis=1, keepdims=True
    )
    x = x_ref[...]
    acts = jnp.dot(x, w_ref[...], preferred_element_type=f32)
    gate, up = acts[:, :hid], acts[:, hid:]
    hidden = (gate / (1.0 + jnp.exp(-gate)) * up * weight).astype(bf16)
    nt = (((1,), (1,)), ((), ()))
    s_gate = lax.dot_general(x, s_ref[:units], nt, preferred_element_type=f32)
    s_up = lax.dot_general(x, s_ref[units:], nt, preferred_element_type=f32)
    s_hidden = (s_gate / (1.0 + jnp.exp(-s_gate)) * s_up).astype(bf16)
    cols = o_ref.shape[1]
    for lo in range(0, cols, 512):
        hi = min(lo + 512, cols)
        o_ref[:, lo:hi] = (
            jnp.dot(hidden, d_ref[:, lo:hi], preferred_element_type=f32)
            + jnp.dot(s_hidden, sd_ref[:, lo:hi], preferred_element_type=f32)
        ).astype(bf16)


def ffn(at, x, w_in, s_in, w_out, s_out):
    rows, width = x.shape
    hid, units, cols = w_in.shape[1] // 2, s_in.shape[0] // 2, w_out.shape[1]
    whole = pl.BlockSpec(memory_space=pltpu.VMEM)
    return pl.pallas_call(
        functools.partial(ffn_kernel, hid=hid, units=units),
        out_shape=jax.ShapeDtypeStruct((rows, cols), bf16),
        in_specs=[pl.BlockSpec(memory_space=pltpu.SMEM)] + [whole] * 5,
        out_specs=whole,
        compiler_params=pltpu.CompilerParams(vmem_limit_bytes=40 * 1024 * 1024),
        cost_estimate=pl.CostEstimate(
            flops=2 * rows * (width * 3 * hid + 2 * hid * cols),
            bytes_accessed=2 * (rows * (width + cols) + width * 2 * hid + hid * cols),
            transcendentals=rows * hid,
        ),
    )(at, x, w_in, s_in, w_out, s_out)


def local(
    tokens,
    gate_codes,
    routes,
    routed_gate,
    routed_up,
    routed_down,
    shared_gate,
    shared_up,
    shared_down,
):
    expert = lax.axis_index(EXPERT)
    part = lax.axis_index(TENSOR)
    toks, width = tokens.shape
    feats = width * L * C
    full = -(-feats // 128) * 128
    n_exp = Y * H * X
    per = n_exp // (L * C)

    gates = gate_codes.astype(f32)
    gates = 2.5 * gates / jnp.sum(gates, axis=1, keepdims=True)
    own = part * per + jnp.arange(per, dtype=jnp.int32)
    table = jnp.sum(jnp.where(routes[:, :, None] == own, gates[:, :, None], 0.0), axis=1)
    high = table.astype(bf16)
    low = (table - high.astype(f32)).astype(bf16)
    sent = jnp.concatenate(
        [tokens, high, low, jnp.zeros((toks, 256 - width - 2 * per), bf16)], 1
    )
    got = lax.all_gather(turn(sent), Z, axis=0, tiled=False)
    got = got.reshape(H, L, toks, 256).transpose(2, 1, 0, 3)
    rows = jnp.concatenate(
        [
            got[..., :width].reshape(toks, feats),
            got[..., width : width + 2 * per].reshape(toks, 2 * n_exp),
            jnp.zeros((toks, full - feats - 2 * n_exp), bf16),
        ],
        1,
    )
    at = (feats - (full - 128) + 2 * per * (expert // per) + expert % per).reshape(1)

    w_gate, w_up, w_down = routed_gate[0], routed_up[0], routed_down[0]
    w_in = jnp.concatenate([w_gate, swap(w_gate), w_up, swap(w_up)], 1)
    w_in = jnp.pad(w_in, ((0, full - feats), (0, 0)))
    w_out = jnp.concatenate([w_down, swap(w_down)], 0)
    units = shared_gate.shape[1] // n_exp
    depth = shared_gate.shape[0]
    s = jnp.stack([shared_gate.T, shared_up.T, shared_down]).reshape(3, n_exp, units, depth)
    s = s.transpose(1, 0, 2, 3).reshape(n_exp, 3 * units, depth)
    s = lax.all_to_all(s, EXPERT, split_axis=0, concat_axis=0, tiled=True)
    s = s.transpose(1, 0, 2).reshape(3, units, feats)
    s = jnp.concatenate([s, swap(s), jnp.zeros((3, 16 - 2 * units, feats), bf16)], 1)
    s_in = jnp.pad(s[:2].reshape(32, feats), ((0, 0), (0, full - feats)))
    s_out = s[2]

    apply = lambda block: ffn(at, block, w_in, s_in, w_out, s_out)

    near = jnp.concatenate([rows, move(rows, 0, 1), move(rows, 0, -1), move(rows, 0, 2)], 0)
    m = near.shape[0] // 2
    prev, succ = move(near, 1, 1), move(near, 1, -1)
    far = jnp.concatenate([move(prev[:m], 1, 1), move(succ[m:], 1, -1)], 0)
    own_out, prev_out, succ_out, far_out = apply(near), apply(prev), apply(succ), apply(far)

    from_prev, from_succ = move(far_out[:m], 1, 1), move(far_out[m:], 1, -1)
    to_succ = jnp.concatenate([add(succ_out[:m], from_prev), succ_out[m:]], 0)
    to_prev = jnp.concatenate([prev_out[:m], add(prev_out[m:], from_succ)], 0)
    total = add(own_out, move(to_succ, 1, 1), move(to_prev, 1, -1))
    total = total.reshape(4, toks, feats)
    total = add(total[0], move(total[1], 0, -1), move(total[2], 0, 1), move(total[3], 0, 2))
    back = total.reshape(toks, L, H, width).transpose(2, 1, 0, 3).reshape(H * L, toks, width)
    back = lax.all_to_all(back, Z, split_axis=0, concat_axis=0, tiled=True)
    return turn(jnp.sum(back.astype(f32), axis=0).astype(bf16))


def solution(mesh):
    fine = Mesh(mesh.devices.reshape(Y, H, X, L, C), AXES)
    in_specs = (
        P(EXPERT, TENSOR),
        P(EXPERT, None),
        P(EXPERT, None),
        P(EXPERT, None, TENSOR),
        P(EXPERT, None, TENSOR),
        P(EXPERT, TENSOR, None),
        P(EXPERT, TENSOR),
        P(EXPERT, TENSOR),
        P(TENSOR, EXPERT),
    )
    return jax.shard_map(
        local, mesh=fine, in_specs=in_specs, out_specs=P(EXPERT, TENSOR), check_vma=False
    )
```

```python
import functools

import jax
import jax.numpy as jnp
from jax import lax
from jax.experimental import pallas as pl
from jax.experimental.pallas import tpu as pltpu
from jax.sharding import Mesh, PartitionSpec as P

Y, H, X, L, C = 4, 2, 4, 8, 2
AXES = ("y", "h", "x", "l", "c")
EXPERT = ("y", "h", "x")
TENSOR = ("l", "c")
Z = ("h", "l")
f32 = jnp.float32
bf16 = jnp.bfloat16


def move(a, stage, k):
    pairs = []
    for y in range(Y):
        for x in range(X):
            for c in range(C):
                to = ((y + k) % Y, x) if (stage + c) % 2 == 0 else (y, (x + k) % X)
                pairs.append(((y * X + x) * C + c, (to[0] * X + to[1]) * C + c))
    return lax.ppermute(a, ("y", "x", "c"), pairs)


def swap(a):
    return lax.ppermute(a, "c", [(0, 1), (1, 0)])


def turn(a):
    return lax.ppermute(a, ("h", "c"), [(h * 2 + c, c * 2 + h) for h in range(2) for c in range(2)])


def add(*terms):
    total = terms[0].astype(f32)
    for t in terms[1:]:
        total = total + t.astype(f32)
    return total.astype(bf16)


def ffn_kernel(at_ref, *refs, hid, parts):
    w_ref, d_ref = refs[parts : parts + 2]
    o_refs = refs[parts + 2 :]
    x = jnp.concatenate([r[...] for r in refs[:parts]], 0)
    width = x.shape[1]
    tail = x[:, width - 128 :].astype(f32)
    lane = lax.broadcasted_iota(jnp.int32, tail.shape, 1)
    at = at_ref[0]
    weight = jnp.sum(
        jnp.where((lane == at) | (lane == at + 2), tail, 0.0), axis=1, keepdims=True
    )
    acts = jnp.dot(x, w_ref[...], preferred_element_type=f32)
    gate, up = acts[:, :hid], acts[:, hid:]
    hidden = (gate / (1.0 + jnp.exp(-gate)) * up * weight).astype(bf16)
    rows = x.shape[0] // parts
    for lo in range(0, width, 512):
        hi = min(lo + 512, width)
        out = jnp.dot(hidden, d_ref[:, lo:hi], preferred_element_type=f32).astype(bf16)
        for i, o_ref in enumerate(o_refs):
            o_ref[:, lo:hi] = out[i * rows : (i + 1) * rows]


def ffn(at, xs, w_in, w_out):
    parts = len(xs)
    rows, width = xs[0].shape
    hid = w_in.shape[1] // 2
    whole = pl.BlockSpec(memory_space=pltpu.VMEM)
    return pl.pallas_call(
        functools.partial(ffn_kernel, hid=hid, parts=parts),
        out_shape=[jax.ShapeDtypeStruct((rows, width), bf16)] * parts,
        in_specs=[pl.BlockSpec(memory_space=pltpu.SMEM)] + [whole] * (parts + 2),
        out_specs=[whole] * parts,
        compiler_params=pltpu.CompilerParams(vmem_limit_bytes=40 * 1024 * 1024),
        cost_estimate=pl.CostEstimate(
            flops=2 * parts * rows * width * 3 * hid,
            bytes_accessed=2 * (2 * parts * rows * width + 3 * width * hid),
            transcendentals=parts * rows * hid,
        ),
    )(at, *xs, w_in, w_out)


def local(
    tokens,
    gate_codes,
    routes,
    routed_gate,
    routed_up,
    routed_down,
    shared_gate,
    shared_up,
    shared_down,
):
    expert = lax.axis_index(EXPERT)
    part = lax.axis_index(TENSOR)
    toks, width = tokens.shape
    feats = width * L * C
    full = -(-feats // 128) * 128
    n_exp = Y * H * X
    per = n_exp // (L * C)

    gates = gate_codes.astype(f32)
    gates = 2.5 * gates / jnp.sum(gates, axis=1, keepdims=True)
    own = part * per + jnp.arange(per, dtype=jnp.int32)
    table = jnp.sum(jnp.where(routes[:, :, None] == own, gates[:, :, None], 0.0), axis=1)
    high = table.astype(bf16)
    low = (table - high.astype(f32)).astype(bf16)
    sent = jnp.concatenate(
        [tokens, high, low, jnp.zeros((toks, 256 - width - 2 * per), bf16)], 1
    )
    got = lax.all_gather(turn(sent), Z, axis=0, tiled=False)
    got = got.reshape(H, L, toks, 256).transpose(2, 1, 0, 3)
    rows = jnp.concatenate(
        [
            got[..., :width].reshape(toks, feats),
            got[..., width : width + 2 * per].reshape(toks, 2 * n_exp),
            jnp.zeros((toks, full - feats - 2 * n_exp), bf16),
        ],
        1,
    )
    at = (feats - (full - 128) + 2 * per * (expert // per) + expert % per).reshape(1)

    w_gate, w_up, w_down = routed_gate[0], routed_up[0], routed_down[0]
    w_in = jnp.concatenate([w_gate, swap(w_gate), w_up, swap(w_up)], 1)
    w_in = jnp.pad(w_in, ((0, full - feats), (0, 0)))
    w_out = jnp.concatenate([w_down, swap(w_down)], 0)
    w_out = jnp.pad(w_out, ((0, 0), (0, full - feats)))

    depth = shared_gate.shape[0]
    s = jnp.concatenate([shared_gate, shared_up, shared_down.T], 0)
    s = jnp.pad(s, ((0, -s.shape[0] % 16), (0, 0)))
    s = lax.all_gather(turn(s), ("y", "c", "x"), axis=0, tiled=False)
    s_gate, s_up, s_down = (
        s[:, i * depth : (i + 1) * depth].reshape(feats, s.shape[2]) for i in range(3)
    )
    s_gate = jnp.dot(rows[:, :feats], s_gate, preferred_element_type=f32)
    s_up = jnp.dot(rows[:, :feats], s_up, preferred_element_type=f32)
    s_hidden = (jax.nn.silu(s_gate) * s_up).astype(bf16)
    shared = lax.dot_general(s_hidden, s_down, (((1,), (1,)), ((), ())), preferred_element_type=f32)

    near = jnp.concatenate([rows, move(rows, 0, 1), move(rows, 0, -1), move(rows, 0, 2)], 0)
    m = near.shape[0] // 2
    prev, succ = move(near, 1, 1), move(near, 1, -1)
    far = [move(prev[:m], 1, 1), move(succ[m:], 1, -1)]
    far_lo, far_hi = ffn(at, far, w_in, w_out)
    (prev_out,), (succ_out,) = ffn(at, [prev], w_in, w_out), ffn(at, [succ], w_in, w_out)
    (own_out,) = ffn(at, [near], w_in, w_out)

    from_prev, from_succ = move(far_lo, 1, 1), move(far_hi, 1, -1)
    to_succ = succ_out.at[:m].set(add(succ_out[:m], from_prev))
    to_prev = prev_out.at[m:].set(add(prev_out[m:], from_succ))
    total = add(own_out, move(to_succ, 1, 1), move(to_prev, 1, -1))
    total = total.reshape(4, toks, full)
    total = [total[0], move(total[1], 0, -1), move(total[2], 0, 1), move(total[3], 0, 2)]
    total = add(shared, *[t[:, :feats] for t in total])
    back = total.reshape(toks, L, H, width).transpose(2, 1, 0, 3).reshape(H * L, toks, width)
    back = lax.all_to_all(back, Z, split_axis=0, concat_axis=0, tiled=True)
    return turn(jnp.sum(back.astype(f32), axis=0).astype(bf16))


def solution(mesh):
    fine = Mesh(mesh.devices.reshape(Y, H, X, L, C), AXES)
    in_specs = (
        P(EXPERT, TENSOR),
        P(EXPERT, None),
        P(EXPERT, None),
        P(EXPERT, None, TENSOR),
        P(EXPERT, None, TENSOR),
        P(EXPERT, TENSOR, None),
        P(EXPERT, TENSOR),
        P(EXPERT, TENSOR),
        P(TENSOR, EXPERT),
    )
    return jax.shard_map(
        local, mesh=fine, in_specs=in_specs, out_specs=P(EXPERT, TENSOR), check_vma=False
    )
```

```python
import functools

import jax
import jax.numpy as jnp
from jax import lax
from jax.experimental import pallas as pl
from jax.experimental.pallas import tpu as pltpu
from jax.sharding import Mesh, PartitionSpec as P

Y, H, X, L, C = 4, 2, 4, 8, 2
AXES = ("y", "h", "x", "l", "c")
EXPERT = ("y", "h", "x")
TENSOR = ("l", "c")
Z = ("h", "l")
f32 = jnp.float32
bf16 = jnp.bfloat16


def move(a, stage, k):
    pairs = []
    for y in range(Y):
        for x in range(X):
            for c in range(C):
                to = ((y + k) % Y, x) if (stage + c) % 2 == 0 else (y, (x + k) % X)
                pairs.append(((y * X + x) * C + c, (to[0] * X + to[1]) * C + c))
    return lax.ppermute(a, ("y", "x", "c"), pairs)


def swap(a):
    return lax.ppermute(a, "c", [(0, 1), (1, 0)])


def turn(a):
    return lax.ppermute(a, ("h", "c"), [(h * 2 + c, c * 2 + h) for h in range(2) for c in range(2)])


def add(*terms):
    total = terms[0].astype(f32)
    for t in terms[1:]:
        total = total + t.astype(f32)
    return total.astype(bf16)


def ffn_kernel(at_ref, *refs, hid, parts):
    w_ref, d_ref = refs[parts : parts + 2]
    o_refs = refs[parts + 2 :]
    x = jnp.concatenate([r[...] for r in refs[:parts]], 0)
    width = x.shape[1]
    tail = x[:, width - 128 :].astype(f32)
    lane = lax.broadcasted_iota(jnp.int32, tail.shape, 1)
    at = at_ref[0]
    weight = jnp.sum(
        jnp.where((lane == at) | (lane == at + 2), tail, 0.0), axis=1, keepdims=True
    )
    acts = jnp.dot(x, w_ref[...], preferred_element_type=f32)
    gate, up = acts[:, :hid], acts[:, hid:]
    hidden = (gate / (1.0 + jnp.exp(-gate)) * up * weight).astype(bf16)
    rows = x.shape[0] // parts
    for lo in range(0, width, 512):
        hi = min(lo + 512, width)
        out = jnp.dot(hidden, d_ref[:, lo:hi], preferred_element_type=f32).astype(bf16)
        for i, o_ref in enumerate(o_refs):
            o_ref[:, lo:hi] = out[i * rows : (i + 1) * rows]


def ffn(at, xs, w_in, w_out):
    parts = len(xs)
    rows, width = xs[0].shape
    hid = w_in.shape[1] // 2
    whole = pl.BlockSpec(memory_space=pltpu.VMEM)
    return pl.pallas_call(
        functools.partial(ffn_kernel, hid=hid, parts=parts),
        out_shape=[jax.ShapeDtypeStruct((rows, width), bf16)] * parts,
        in_specs=[pl.BlockSpec(memory_space=pltpu.SMEM)] + [whole] * (parts + 2),
        out_specs=[whole] * parts,
        compiler_params=pltpu.CompilerParams(vmem_limit_bytes=40 * 1024 * 1024),
        cost_estimate=pl.CostEstimate(
            flops=2 * parts * rows * width * 3 * hid,
            bytes_accessed=2 * (2 * parts * rows * width + 3 * width * hid),
            transcendentals=parts * rows * hid,
        ),
    )(at, *xs, w_in, w_out)


def local(
    tokens,
    gate_codes,
    routes,
    routed_gate,
    routed_up,
    routed_down,
    shared_gate,
    shared_up,
    shared_down,
):
    expert = lax.axis_index(EXPERT)
    part = lax.axis_index(TENSOR)
    core = lax.axis_index("c")
    toks, width = tokens.shape
    feats = width * L * C
    full = -(-feats // 128) * 128
    n_exp = Y * H * X
    per = n_exp // (L * C)

    gates = gate_codes.astype(f32)
    gates = 2.5 * gates / jnp.sum(gates, axis=1, keepdims=True)
    own = part * per + jnp.arange(per, dtype=jnp.int32)
    table = jnp.sum(jnp.where(routes[:, :, None] == own, gates[:, :, None], 0.0), axis=1)
    high = table.astype(bf16)
    low = (table - high.astype(f32)).astype(bf16)
    sent = jnp.concatenate([high, low, jnp.zeros((toks, 256 - width - 2 * per), bf16)], 1)
    sent = jnp.concatenate([tokens, sent], 1)
    half = toks // C
    sent = jnp.concatenate(
        [
            lax.dynamic_slice_in_dim(sent, core * half, half, 0),
            swap(lax.dynamic_slice_in_dim(sent, (1 - core) * half, half, 0)),
        ],
        1,
    )
    got = lax.all_gather(sent, Z, axis=0, tiled=False)
    got = got.reshape(H, L, half, C, 256)
    got = jnp.where(core == 0, got, got[:, :, :, ::-1]).transpose(0, 2, 1, 3, 4)
    rows = jnp.concatenate(
        [
            got[..., :width].reshape(toks, feats),
            got[..., width : width + 2 * per].reshape(toks, 2 * n_exp),
            jnp.zeros((toks, full - feats - 2 * n_exp), bf16),
        ],
        1,
    )
    at = (feats - (full - 128) + 2 * per * (expert // per) + expert % per).reshape(1)

    w_gate, w_up, w_down = routed_gate[0], routed_up[0], routed_down[0]
    w_in = jnp.concatenate([w_gate, swap(w_gate), w_up, swap(w_up)], 1)
    w_in = jnp.pad(w_in, ((0, full - feats), (0, 0)))
    w_out = jnp.concatenate([w_down, swap(w_down)], 0)
    w_out = jnp.pad(w_out, ((0, 0), (0, full - feats)))

    depth = shared_gate.shape[0]
    s = jnp.concatenate([shared_gate, shared_up, shared_down.T], 0)
    s = jnp.pad(s, ((0, -s.shape[0] % 16), (0, 0)))
    rows, s = lax.optimization_barrier((rows, turn(s)))
    s = lax.all_gather(s, ("y", "c", "x"), axis=0, tiled=False)
    s_gate, s_up, s_down = (
        s[:, i * depth : (i + 1) * depth].reshape(feats, s.shape[2]) for i in range(3)
    )
    s_gate = jnp.dot(rows[:, :feats], s_gate, preferred_element_type=f32)
    s_up = jnp.dot(rows[:, :feats], s_up, preferred_element_type=f32)
    s_hidden = (jax.nn.silu(s_gate) * s_up).astype(bf16)
    shared = lax.dot_general(s_hidden, s_down, (((1,), (1,)), ((), ())), preferred_element_type=f32)

    apply = lambda *blocks: ffn(at, blocks, w_in, w_out)
    lo = jnp.concatenate([rows, move(rows, 0, 1)], 0)
    hi = jnp.concatenate([move(rows, 0, -1), move(rows, 0, 2)], 0)
    prev_lo, succ_hi = move(lo, 1, 1), move(hi, 1, -1)
    prev_hi, succ_lo = move(hi, 1, 1), move(lo, 1, -1)
    far_lo, far_hi = apply(move(prev_lo, 1, 1), move(succ_hi, 1, -1))

    from_prev, from_succ = move(far_lo, 1, 1), move(far_hi, 1, -1)
    prev_lo, prev_hi = apply(prev_lo, prev_hi)
    succ_lo, succ_hi = apply(succ_lo, succ_hi)
    prev_lo, succ_hi = move(prev_lo, 1, -1), move(succ_hi, 1, 1)
    lo, hi, shared = lax.optimization_barrier((lo, hi, shared))
    own_lo, own_hi = apply(lo, hi)
    prev_hi = move(add(prev_hi, from_succ), 1, -1)
    succ_lo = move(add(succ_lo, from_prev), 1, 1)
    los, his = (own_lo, prev_lo, succ_lo), (own_hi, prev_hi, succ_hi)
    total = [t[:toks] for t in los]
    total.append(move(add(*[t[toks:] for t in los]), 0, -1))
    total.append(move(add(*[t[:toks] for t in his]), 0, 1))
    total.append(move(add(*[t[toks:] for t in his]), 0, 2))
    total = add(shared, *[t[:, :feats] for t in total])

    back = total.reshape(H, half, L, C, width).transpose(0, 2, 3, 1, 4)
    back = jnp.where(core == 0, back, back[:, :, ::-1])
    back = back.reshape(H * L, C * half, width)
    back = lax.all_to_all(back, Z, split_axis=0, concat_axis=0, tiled=True)
    done = jnp.sum(back.astype(f32), axis=0).astype(bf16)
    keep, take = done[:half], swap(done[half:])
    return jnp.where(
        core == 0, jnp.concatenate([keep, take], 0), jnp.concatenate([take, keep], 0)
    )


def solution(mesh):
    fine = Mesh(mesh.devices.reshape(Y, H, X, L, C), AXES)
    in_specs = (
        P(EXPERT, TENSOR),
        P(EXPERT, None),
        P(EXPERT, None),
        P(EXPERT, None, TENSOR),
        P(EXPERT, None, TENSOR),
        P(EXPERT, TENSOR, None),
        P(EXPERT, TENSOR),
        P(EXPERT, TENSOR),
        P(TENSOR, EXPERT),
    )
    return jax.shard_map(
        local, mesh=fine, in_specs=in_specs, out_specs=P(EXPERT, TENSOR), check_vma=False
    )
```

```python
import functools

import jax
import jax.numpy as jnp
from jax import lax
from jax.experimental import pallas as pl
from jax.experimental.pallas import tpu as pltpu
from jax.sharding import Mesh, PartitionSpec as P

Y, H, X, L, C = 4, 2, 4, 8, 2
AXES = ("y", "h", "x", "l", "c")
EXPERT = ("y", "h", "x")
TENSOR = ("l", "c")
Z = ("h", "l")
f32 = jnp.float32
bf16 = jnp.bfloat16


def move(a, stage, k):
    pairs = []
    for y in range(Y):
        for x in range(X):
            for c in range(C):
                to = ((y + k) % Y, x) if (stage + c) % 2 == 0 else (y, (x + k) % X)
                pairs.append(((y * X + x) * C + c, (to[0] * X + to[1]) * C + c))
    return lax.ppermute(a, ("y", "x", "c"), pairs)


def swap(a):
    return lax.ppermute(a, "c", [(0, 1), (1, 0)])


def spread(a):
    groups = [[(y * X + x) * C for y in range(Y)] for x in range(X)]
    groups += [[(y * X + x) * C + 1 for x in range(X)] for y in range(Y)]
    return lax.all_to_all(
        a, ("y", "x", "c"), 0, 0, axis_index_groups=groups, tiled=True
    )


def turn(a):
    return lax.ppermute(a, ("h", "c"), [(h * 2 + c, c * 2 + h) for h in range(2) for c in range(2)])


def add(*terms):
    total = terms[0].astype(f32)
    for t in terms[1:]:
        total = total + t.astype(f32)
    return total.astype(bf16)


def ffn_kernel(at_ref, *refs, hid, parts):
    w_ref, d_ref = refs[parts : parts + 2]
    o_refs = refs[parts + 2 :]
    x = jnp.concatenate([r[...] for r in refs[:parts]], 0)
    width = x.shape[1]
    tail = x[:, width - 128 :].astype(f32)
    lane = lax.broadcasted_iota(jnp.int32, tail.shape, 1)
    at = at_ref[0]
    weight = jnp.sum(
        jnp.where((lane == at) | (lane == at + 2), tail, 0.0), axis=1, keepdims=True
    )
    acts = jnp.dot(x, w_ref[...], preferred_element_type=f32)
    gate, up = acts[:, :hid], acts[:, hid:]
    hidden = (gate / (1.0 + jnp.exp(-gate)) * up * weight).astype(bf16)
    rows = x.shape[0] // parts
    for lo in range(0, width, 512):
        hi = min(lo + 512, width)
        out = jnp.dot(hidden, d_ref[:, lo:hi], preferred_element_type=f32).astype(bf16)
        for i, o_ref in enumerate(o_refs):
            o_ref[:, lo:hi] = out[i * rows : (i + 1) * rows]


def ffn(at, xs, w_in, w_out):
    parts = len(xs)
    rows, width = xs[0].shape
    hid = w_in.shape[1] // 2
    whole = pl.BlockSpec(memory_space=pltpu.VMEM)
    return pl.pallas_call(
        functools.partial(ffn_kernel, hid=hid, parts=parts),
        out_shape=[jax.ShapeDtypeStruct((rows, width), bf16)] * parts,
        in_specs=[pl.BlockSpec(memory_space=pltpu.SMEM)] + [whole] * (parts + 2),
        out_specs=[whole] * parts,
        compiler_params=pltpu.CompilerParams(vmem_limit_bytes=40 * 1024 * 1024),
        cost_estimate=pl.CostEstimate(
            flops=2 * parts * rows * width * 3 * hid,
            bytes_accessed=2 * (2 * parts * rows * width + 3 * width * hid),
            transcendentals=parts * rows * hid,
        ),
    )(at, *xs, w_in, w_out)


def local(
    tokens,
    gate_codes,
    routes,
    routed_gate,
    routed_up,
    routed_down,
    shared_gate,
    shared_up,
    shared_down,
):
    expert = lax.axis_index(EXPERT)
    part = lax.axis_index(TENSOR)
    core = lax.axis_index("c")
    toks, width = tokens.shape
    feats = width * L * C
    full = -(-feats // 128) * 128
    n_exp = Y * H * X
    per = n_exp // (L * C)

    gates = gate_codes.astype(f32)
    gates = 2.5 * gates / jnp.sum(gates, axis=1, keepdims=True)
    own = part * per + jnp.arange(per, dtype=jnp.int32)
    table = jnp.sum(jnp.where(routes[:, :, None] == own, gates[:, :, None], 0.0), axis=1)
    high = table.astype(bf16)
    low = (table - high.astype(f32)).astype(bf16)
    sent = jnp.concatenate([high, low, jnp.zeros((toks, 256 - width - 2 * per), bf16)], 1)
    sent = jnp.concatenate([tokens, sent], 1)
    half = toks // C
    sent = jnp.concatenate(
        [
            lax.dynamic_slice_in_dim(sent, core * half, half, 0),
            swap(lax.dynamic_slice_in_dim(sent, (1 - core) * half, half, 0)),
        ],
        1,
    )
    got = lax.all_gather(sent, Z, axis=0, tiled=False)
    got = got.reshape(H, L, half, C, 256)
    got = jnp.where(core == 0, got, got[:, :, :, ::-1]).transpose(0, 2, 1, 3, 4)
    rows = jnp.concatenate(
        [
            got[..., :width].reshape(toks, feats),
            got[..., width : width + 2 * per].reshape(toks, 2 * n_exp),
            jnp.zeros((toks, full - feats - 2 * n_exp), bf16),
        ],
        1,
    )
    at = (feats - (full - 128) + 2 * per * (expert // per) + expert % per).reshape(1)

    w_gate, w_up, w_down = routed_gate[0], routed_up[0], routed_down[0]
    w_in = jnp.concatenate([w_gate, swap(w_gate), w_up, swap(w_up)], 1)
    w_in = jnp.pad(w_in, ((0, full - feats), (0, 0)))
    w_out = jnp.concatenate([w_down, swap(w_down)], 0)
    w_out = jnp.pad(w_out, ((0, 0), (0, full - feats)))

    depth = shared_gate.shape[0]
    s = jnp.concatenate([shared_gate, shared_up, shared_down.T], 0)
    s = jnp.pad(s, ((0, -s.shape[0] % 16), (0, 0)))
    rows, s = lax.optimization_barrier((rows, turn(s)))
    s = lax.all_gather(s, ("y", "c", "x"), axis=0, tiled=False)
    s_gate, s_up, s_down = (
        s[:, i * depth : (i + 1) * depth].reshape(feats, s.shape[2]) for i in range(3)
    )
    s_gate = jnp.dot(rows[:, :feats], s_gate, preferred_element_type=f32)
    s_up = jnp.dot(rows[:, :feats], s_up, preferred_element_type=f32)
    s_hidden = (jax.nn.silu(s_gate) * s_up).astype(bf16)
    shared = lax.dot_general(s_hidden, s_down, (((1,), (1,)), ((), ())), preferred_element_type=f32)

    apply = lambda *blocks: ffn(at, blocks, w_in, w_out)
    order = lax.optimization_barrier
    near = spread(jnp.concatenate([rows] * 4, 0))
    lo, hi = near[: 2 * toks], near[2 * toks :]
    prev_lo, succ_hi = move(lo, 1, 1), move(hi, 1, -1)
    far = move(prev_lo, 1, 1), move(succ_hi, 1, -1)
    prev_lo, succ_hi = apply(prev_lo, succ_hi)
    lo, hi, prev_lo, succ_hi = order((lo, hi, prev_lo, succ_hi))
    prev_hi, succ_lo = move(hi, 1, 1), move(lo, 1, -1)
    back_p, back_s = move(prev_lo, 1, -1), move(succ_hi, 1, 1)
    far_lo, far_hi = apply(*far)

    far_lo, far_hi, prev_hi, succ_lo = order((far_lo, far_hi, prev_hi, succ_lo))
    from_prev, from_succ = move(far_lo, 1, 1), move(far_hi, 1, -1)
    prev_hi, succ_lo = apply(prev_hi, succ_lo)
    lo, hi, shared, prev_hi, succ_lo = order((lo, hi, shared, prev_hi, succ_lo))
    own_lo, own_hi = apply(lo, hi)
    prev_hi = move(add(prev_hi, from_succ), 1, -1)
    succ_lo = move(add(succ_lo, from_prev), 1, 1)
    total = jnp.concatenate([add(own_lo, back_p, succ_lo), add(own_hi, back_s, prev_hi)], 0)
    total = spread(total)
    total = [total[i * toks : (i + 1) * toks] for i in range(4)]
    total = add(shared, *[t[:, :feats] for t in total])

    back = total.reshape(H, half, L, C, width).transpose(0, 2, 3, 1, 4)
    back = jnp.where(core == 0, back, back[:, :, ::-1])
    back = back.reshape(H * L, C * half, width)
    back = lax.all_to_all(back, Z, split_axis=0, concat_axis=0, tiled=True)
    done = jnp.sum(back.astype(f32), axis=0).astype(bf16)
    keep, take = done[:half], swap(done[half:])
    return jnp.where(
        core == 0, jnp.concatenate([keep, take], 0), jnp.concatenate([take, keep], 0)
    )


def solution(mesh):
    fine = Mesh(mesh.devices.reshape(Y, H, X, L, C), AXES)
    in_specs = (
        P(EXPERT, TENSOR),
        P(EXPERT, None),
        P(EXPERT, None),
        P(EXPERT, None, TENSOR),
        P(EXPERT, None, TENSOR),
        P(EXPERT, TENSOR, None),
        P(EXPERT, TENSOR),
        P(EXPERT, TENSOR),
        P(TENSOR, EXPERT),
    )
    return jax.shard_map(
        local, mesh=fine, in_specs=in_specs, out_specs=P(EXPERT, TENSOR), check_vma=False
    )
```

```python
import functools

import jax
import jax.numpy as jnp
from jax import lax
from jax.experimental import pallas as pl
from jax.experimental.pallas import tpu as pltpu
from jax.sharding import Mesh, PartitionSpec as P

Y, H, X, L, C = 4, 2, 4, 8, 2
AXES = ("y", "h", "x", "l", "c")
EXPERT = ("y", "h", "x")
TENSOR = ("l", "c")
Z = ("h", "l")
f32 = jnp.float32
bf16 = jnp.bfloat16


def move(a, stage, k):
    pairs = []
    for y in range(Y):
        for x in range(X):
            for c in range(C):
                to = ((y + k) % Y, x) if (stage + c) % 2 == 0 else (y, (x + k) % X)
                pairs.append(((y * X + x) * C + c, (to[0] * X + to[1]) * C + c))
    return lax.ppermute(a, ("y", "x", "c"), pairs)


def swap(a):
    return lax.ppermute(a, "c", [(0, 1), (1, 0)])


def spread(a):
    groups = [[(y * X + x) * C for y in range(Y)] for x in range(X)]
    groups += [[(y * X + x) * C + 1 for x in range(X)] for y in range(Y)]
    return lax.all_to_all(
        a, ("y", "x", "c"), 0, 0, axis_index_groups=groups, tiled=True
    )


def add(*terms):
    total = terms[0].astype(f32)
    for t in terms[1:]:
        total = total + t.astype(f32)
    return total.astype(bf16)


def ffn_kernel(at_ref, *refs, hid, parts):
    w_ref, d_ref = refs[parts : parts + 2]
    o_refs = refs[parts + 2 :]
    x = jnp.concatenate([r[...] for r in refs[:parts]], 0)
    width = x.shape[1]
    tail = x[:, width - 128 :].astype(f32)
    lane = lax.broadcasted_iota(jnp.int32, tail.shape, 1)
    at = at_ref[0]
    weight = jnp.sum(
        jnp.where((lane == at) | (lane == at + 2), tail, 0.0), axis=1, keepdims=True
    )
    acts = jnp.dot(x, w_ref[...], preferred_element_type=f32)
    gate, up = acts[:, :hid], acts[:, hid:]
    hidden = (gate / (1.0 + jnp.exp(-gate)) * up * weight).astype(bf16)
    rows = x.shape[0] // parts
    for lo in range(0, width, 512):
        hi = min(lo + 512, width)
        out = jnp.dot(hidden, d_ref[:, lo:hi], preferred_element_type=f32).astype(bf16)
        for i, o_ref in enumerate(o_refs):
            o_ref[:, lo:hi] = out[i * rows : (i + 1) * rows]


def ffn(at, xs, w_in, w_out):
    parts = len(xs)
    rows, width = xs[0].shape
    hid = w_in.shape[1] // 2
    whole = pl.BlockSpec(memory_space=pltpu.VMEM)
    return pl.pallas_call(
        functools.partial(ffn_kernel, hid=hid, parts=parts),
        out_shape=[jax.ShapeDtypeStruct((rows, width), bf16)] * parts,
        in_specs=[pl.BlockSpec(memory_space=pltpu.SMEM)] + [whole] * (parts + 2),
        out_specs=[whole] * parts,
        compiler_params=pltpu.CompilerParams(vmem_limit_bytes=40 * 1024 * 1024),
        cost_estimate=pl.CostEstimate(
            flops=2 * parts * rows * width * 3 * hid,
            bytes_accessed=2 * (2 * parts * rows * width + 3 * width * hid),
            transcendentals=parts * rows * hid,
        ),
    )(at, *xs, w_in, w_out)


def rows_kernel(core_ref, got_ref, o_ref, *, width, extra):
    core = core_ref[0]
    half = got_ref.shape[1]
    for h in range(H):
        own, other, pieces = [], [], []
        for block in range(L):
            v = got_ref[h * L + block]
            own.append(v[:, :256].astype(f32))
            other.append(v[:, 256:].astype(f32))
        for block in range(L):
            pieces.append(jnp.where(core == 0, own[block], other[block]))
            pieces.append(jnp.where(core == 0, other[block], own[block]))
        feats = width * len(pieces)
        used = feats + extra * len(pieces)
        row = jnp.concatenate(
            [p[:, :width] for p in pieces]
            + [p[:, width : width + extra] for p in pieces]
            + [jnp.zeros((half, o_ref.shape[1] - used), f32)],
            1,
        ).astype(bf16)
        for copy in range(o_ref.shape[0] // (H * half)):
            at = (copy * H + h) * half
            o_ref[at : at + half, :] = row


def assemble(core, got, width, extra, full):
    return pl.pallas_call(
        functools.partial(rows_kernel, width=width, extra=extra),
        out_shape=jax.ShapeDtypeStruct((4 * H * got.shape[1], full), bf16),
        in_specs=[
            pl.BlockSpec(memory_space=pltpu.SMEM),
            pl.BlockSpec(memory_space=pltpu.VMEM),
        ],
        out_specs=pl.BlockSpec(memory_space=pltpu.VMEM),
        compiler_params=pltpu.CompilerParams(vmem_limit_bytes=32 * 1024 * 1024),
        cost_estimate=pl.CostEstimate(flops=0, bytes_accessed=3_000_000, transcendentals=0),
    )(core.reshape(1), got)


def shared_kernel(x_ref, s_ref, o_ref, *, depth):
    count = s_ref.shape[0]
    gate = jnp.zeros((x_ref.shape[0], 128), f32)
    up = gate
    for e in range(count):
        x = x_ref[:, e * depth : e * depth + 128]
        gate += jnp.dot(x, s_ref[e, :128, :], preferred_element_type=f32)
        up += jnp.dot(x, s_ref[e, 128:256, :], preferred_element_type=f32)
    hidden = (gate / (1.0 + jnp.exp(-gate)) * up).astype(bf16)
    outs = []
    for e in range(count):
        out = lax.dot_general(
            hidden, s_ref[e, 256:384, :], (((1,), (1,)), ((), ())), preferred_element_type=f32
        )
        outs.append(out[:, :depth])
    o_ref[...] = jnp.concatenate(outs, 1)


def shared_expert(x, s, depth):
    rows, count = x.shape[0], s.shape[0]
    whole = pl.BlockSpec(memory_space=pltpu.VMEM)
    return pl.pallas_call(
        functools.partial(shared_kernel, depth=depth),
        out_shape=jax.ShapeDtypeStruct((rows, count * depth), f32),
        in_specs=[whole] * 2,
        out_specs=whole,
        compiler_params=pltpu.CompilerParams(vmem_limit_bytes=32 * 1024 * 1024),
        cost_estimate=pl.CostEstimate(
            flops=6 * rows * count * 128 * 128, bytes_accessed=6_000_000, transcendentals=rows * 128
        ),
    )(x, s)


def local(
    tokens,
    gate_codes,
    routes,
    routed_gate,
    routed_up,
    routed_down,
    shared_gate,
    shared_up,
    shared_down,
):
    expert = lax.axis_index(EXPERT)
    part = lax.axis_index(TENSOR)
    core = lax.axis_index("c")
    order = lax.optimization_barrier
    toks, width = tokens.shape
    feats = width * L * C
    full = -(-feats // 128) * 128
    n_exp = Y * H * X
    per = n_exp // (L * C)

    gates = gate_codes.astype(f32)
    gates = 2.5 * gates / jnp.sum(gates, axis=1, keepdims=True)
    own = part * per + jnp.arange(per, dtype=jnp.int32)
    table = jnp.sum(jnp.where(routes[:, :, None] == own, gates[:, :, None], 0.0), axis=1)
    high = table.astype(bf16)
    low = (table - high.astype(f32)).astype(bf16)
    sent = jnp.concatenate([high, low, jnp.zeros((toks, 256 - width - 2 * per), bf16)], 1)
    sent = jnp.concatenate([tokens, sent], 1)
    half = toks // C
    sent = jnp.concatenate(
        [
            lax.dynamic_slice_in_dim(sent, core * half, half, 0),
            swap(lax.dynamic_slice_in_dim(sent, (1 - core) * half, half, 0)),
        ],
        1,
    )
    s = jnp.stack([shared_gate, shared_up, shared_down.T])
    depth = s.shape[1]
    s = jnp.pad(s, ((0, 0), (0, 128 - depth), (0, 0))).reshape(384, 128)
    sent, s = order((sent, s))
    s = lax.all_gather(s, EXPERT, axis=0, tiled=False)
    got = lax.all_gather(sent, Z, axis=0, tiled=False)
    copies = assemble(core, got, width, 2 * per, full)
    at = (feats - (full - 128) + 2 * per * (expert // per) + expert % per).reshape(1)

    w_gate, w_up, w_down = routed_gate[0], routed_up[0], routed_down[0]
    w_in = jnp.concatenate([w_gate, swap(w_gate), w_up, swap(w_up)], 1)
    w_in = jnp.pad(w_in, ((0, full - feats), (0, 0)))
    w_out = jnp.concatenate([w_down, swap(w_down)], 0)
    w_out = jnp.pad(w_out, ((0, 0), (0, full - feats)))

    apply = lambda *blocks: ffn(at, blocks, w_in, w_out)
    held = lax.dynamic_slice_in_dim(copies, lax.axis_index("h") * half, half, 0)
    near, held = order((spread(copies), jnp.concatenate([held, swap(held)], 0)))
    lo, hi = near[: 2 * toks], near[2 * toks :]
    prev_lo, succ_hi = move(lo, 1, 1), move(hi, 1, -1)
    far_lo, far_hi, s = order((move(prev_lo, 1, 1), move(succ_hi, 1, -1), s))
    prev_lo, succ_hi = apply(prev_lo, succ_hi)
    lo, hi, prev_lo, succ_hi = order((lo, hi, prev_lo, succ_hi))
    prev_hi, succ_lo = move(hi, 1, 1), move(lo, 1, -1)
    back_p, back_s = move(prev_lo, 1, -1), move(succ_hi, 1, 1)
    far_lo, far_hi = apply(far_lo, far_hi)

    far_lo, far_hi, prev_hi, succ_lo = order((far_lo, far_hi, prev_hi, succ_lo))
    from_prev, from_succ = move(far_lo, 1, 1), move(far_hi, 1, -1)
    prev_hi, succ_lo = apply(prev_hi, succ_lo)
    prev_hi, succ_lo, s = order((prev_hi, succ_lo, s))
    out = shared_expert(held, s, depth)
    prev_hi, succ_lo = add(prev_hi, from_succ), add(succ_lo, from_prev)
    prev_hi, succ_lo, lo, hi, out, back_p, back_s = order(
        (prev_hi, succ_lo, lo, hi, out, back_p, back_s)
    )
    prev_hi, succ_lo = move(prev_hi, 1, -1), move(succ_lo, 1, 1)
    own_lo, own_hi = apply(lo, hi)
    out = out[:half] + swap(out[half:].astype(bf16)).astype(f32)
    here = jnp.arange(H * half, dtype=jnp.int32)[:, None] // half == lax.axis_index("h")
    shared = jnp.where(here, jnp.concatenate([out] * H, 0), 0.0)
    total = jnp.concatenate([add(own_lo, back_p, succ_lo), add(own_hi, back_s, prev_hi)], 0)
    total = spread(total)
    total = [total[i * toks : (i + 1) * toks] for i in range(4)]
    total = add(shared, *[t[:, :feats] for t in total])

    back = total.reshape(H, half, L, C, width).transpose(0, 2, 3, 1, 4)
    back = jnp.where(core == 0, back, back[:, :, ::-1])
    back = back.reshape(H * L, C * half, width)
    back = lax.all_to_all(back, Z, split_axis=0, concat_axis=0, tiled=True)
    done = jnp.sum(back.astype(f32), axis=0).astype(bf16)
    keep, take = done[:half], swap(done[half:])
    return jnp.where(
        core == 0, jnp.concatenate([keep, take], 0), jnp.concatenate([take, keep], 0)
    )


def solution(mesh):
    fine = Mesh(mesh.devices.reshape(Y, H, X, L, C), AXES)
    in_specs = (
        P(EXPERT, TENSOR),
        P(EXPERT, None),
        P(EXPERT, None),
        P(EXPERT, None, TENSOR),
        P(EXPERT, None, TENSOR),
        P(EXPERT, TENSOR, None),
        P(EXPERT, TENSOR),
        P(EXPERT, TENSOR),
        P(TENSOR, EXPERT),
    )
    return jax.shard_map(
        local, mesh=fine, in_specs=in_specs, out_specs=P(EXPERT, TENSOR), check_vma=False
    )
```

```python
import functools

import jax
import jax.numpy as jnp
from jax import lax
from jax.experimental import pallas as pl
from jax.experimental.pallas import tpu as pltpu
from jax.sharding import Mesh, PartitionSpec as P

Y, H, X, L, C = 4, 2, 4, 8, 2
AXES = ("y", "h", "x", "l", "c")
EXPERT = ("y", "h", "x")
TENSOR = ("l", "c")
Z = ("h", "l")
f32 = jnp.float32
bf16 = jnp.bfloat16


def move(a, stage, k):
    pairs = []
    for y in range(Y):
        for x in range(X):
            for c in range(C):
                to = ((y + k) % Y, x) if (stage + c) % 2 == 0 else (y, (x + k) % X)
                pairs.append(((y * X + x) * C + c, (to[0] * X + to[1]) * C + c))
    return lax.ppermute(a, ("y", "x", "c"), pairs)


def swap(a):
    return lax.ppermute(a, "c", [(0, 1), (1, 0)])


def spread(a):
    groups = [[(y * X + x) * C for y in range(Y)] for x in range(X)]
    groups += [[(y * X + x) * C + 1 for x in range(X)] for y in range(Y)]
    return lax.all_to_all(
        a, ("y", "x", "c"), 0, 0, axis_index_groups=groups, tiled=True
    )


def add(*terms):
    total = terms[0].astype(f32)
    for t in terms[1:]:
        total = total + t.astype(f32)
    return total.astype(bf16)


def ffn_kernel(at_ref, *refs, hid, parts):
    w_ref, d_ref = refs[parts : parts + 2]
    o_refs = refs[parts + 2 :]
    x = jnp.concatenate([r[...] for r in refs[:parts]], 0)
    width = x.shape[1]
    tail = x[:, width - 128 :].astype(f32)
    lane = lax.broadcasted_iota(jnp.int32, tail.shape, 1)
    at = at_ref[0]
    weight = jnp.sum(
        jnp.where((lane == at) | (lane == at + 2), tail, 0.0), axis=1, keepdims=True
    )
    acts = jnp.dot(x, w_ref[...], preferred_element_type=f32)
    gate, up = acts[:, :hid], acts[:, hid:]
    hidden = (gate / (1.0 + jnp.exp(-gate)) * up * weight).astype(bf16)
    rows = x.shape[0] // parts
    for lo in range(0, width, 512):
        hi = min(lo + 512, width)
        out = jnp.dot(hidden, d_ref[:, lo:hi], preferred_element_type=f32).astype(bf16)
        for i, o_ref in enumerate(o_refs):
            o_ref[:, lo:hi] = out[i * rows : (i + 1) * rows]


def ffn(at, xs, w_in, w_out):
    parts = len(xs)
    rows, width = xs[0].shape
    hid = w_in.shape[1] // 2
    whole = pl.BlockSpec(memory_space=pltpu.VMEM)
    return pl.pallas_call(
        functools.partial(ffn_kernel, hid=hid, parts=parts),
        out_shape=[jax.ShapeDtypeStruct((rows, width), bf16)] * parts,
        in_specs=[pl.BlockSpec(memory_space=pltpu.SMEM)] + [whole] * (parts + 2),
        out_specs=[whole] * parts,
        compiler_params=pltpu.CompilerParams(vmem_limit_bytes=40 * 1024 * 1024),
        cost_estimate=pl.CostEstimate(
            flops=2 * parts * rows * width * 3 * hid,
            bytes_accessed=2 * (2 * parts * rows * width + 3 * width * hid),
            transcendentals=parts * rows * hid,
        ),
    )(at, *xs, w_in, w_out)


def rows_kernel(core_ref, got_ref, o_ref, *, width, extra):
    core = core_ref[0]
    half = got_ref.shape[1]
    for h in range(H):
        own, other, pieces = [], [], []
        for block in range(L):
            v = got_ref[h * L + block]
            own.append(v[:, :256].astype(f32))
            other.append(v[:, 256:].astype(f32))
        for block in range(L):
            pieces.append(jnp.where(core == 0, own[block], other[block]))
            pieces.append(jnp.where(core == 0, other[block], own[block]))
        feats = width * len(pieces)
        used = feats + extra * len(pieces)
        row = jnp.concatenate(
            [p[:, :width] for p in pieces]
            + [p[:, width : width + extra] for p in pieces]
            + [jnp.zeros((half, o_ref.shape[1] - used), f32)],
            1,
        ).astype(bf16)
        for copy in range(o_ref.shape[0] // (H * half)):
            at = (copy * H + h) * half
            o_ref[at : at + half, :] = row


def assemble(core, got, width, extra, full):
    return pl.pallas_call(
        functools.partial(rows_kernel, width=width, extra=extra),
        out_shape=jax.ShapeDtypeStruct((4 * H * got.shape[1], full), bf16),
        in_specs=[
            pl.BlockSpec(memory_space=pltpu.SMEM),
            pl.BlockSpec(memory_space=pltpu.VMEM),
        ],
        out_specs=pl.BlockSpec(memory_space=pltpu.VMEM),
        compiler_params=pltpu.CompilerParams(vmem_limit_bytes=32 * 1024 * 1024),
        cost_estimate=pl.CostEstimate(flops=0, bytes_accessed=3_000_000, transcendentals=0),
    )(core.reshape(1), got)


def shared_kernel(x_ref, s_ref, o_ref, *, depth):
    count = s_ref.shape[0]
    gate = jnp.zeros((x_ref.shape[0], 128), f32)
    up = gate
    at = [(e // X % H * Y + e // X // H) * X + e % X for e in range(count)]
    for e in range(count):
        x = x_ref[:, e * depth : e * depth + 128]
        gate += jnp.dot(x, s_ref[at[e], :128, :], preferred_element_type=f32)
        up += jnp.dot(x, s_ref[at[e], 128:256, :], preferred_element_type=f32)
    hidden = (gate / (1.0 + jnp.exp(-gate)) * up).astype(bf16)
    outs = []
    for e in range(count):
        out = lax.dot_general(
            hidden, s_ref[at[e], 256:384, :], (((1,), (1,)), ((), ())), preferred_element_type=f32
        )
        outs.append(out[:, :depth])
    o_ref[...] = jnp.concatenate(outs, 1)


def shared_expert(x, s, depth):
    rows, count = x.shape[0], s.shape[0]
    whole = pl.BlockSpec(memory_space=pltpu.VMEM)
    return pl.pallas_call(
        functools.partial(shared_kernel, depth=depth),
        out_shape=jax.ShapeDtypeStruct((rows, count * depth), f32),
        in_specs=[whole] * 2,
        out_specs=whole,
        compiler_params=pltpu.CompilerParams(vmem_limit_bytes=32 * 1024 * 1024),
        cost_estimate=pl.CostEstimate(
            flops=6 * rows * count * 128 * 128, bytes_accessed=6_000_000, transcendentals=rows * 128
        ),
    )(x, s)


def local(
    tokens,
    gate_codes,
    routes,
    routed_gate,
    routed_up,
    routed_down,
    shared_gate,
    shared_up,
    shared_down,
):
    expert = lax.axis_index(EXPERT)
    part = lax.axis_index(TENSOR)
    core = lax.axis_index("c")
    order = lax.optimization_barrier
    toks, width = tokens.shape
    feats = width * L * C
    full = -(-feats // 128) * 128
    n_exp = Y * H * X
    per = n_exp // (L * C)

    gates = gate_codes.astype(f32)
    gates = 2.5 * gates / jnp.sum(gates, axis=1, keepdims=True)
    own = part * per + jnp.arange(per, dtype=jnp.int32)
    table = jnp.sum(jnp.where(routes[:, :, None] == own, gates[:, :, None], 0.0), axis=1)
    high = table.astype(bf16)
    low = (table - high.astype(f32)).astype(bf16)
    sent = jnp.concatenate([high, low, jnp.zeros((toks, 256 - width - 2 * per), bf16)], 1)
    sent = jnp.concatenate([tokens, sent], 1)
    half = toks // C
    sent = jnp.concatenate(
        [
            lax.dynamic_slice_in_dim(sent, core * half, half, 0),
            swap(lax.dynamic_slice_in_dim(sent, (1 - core) * half, half, 0)),
        ],
        1,
    )
    s = jnp.stack([shared_gate, shared_up, shared_down.T])
    depth = s.shape[1]
    s = jnp.pad(s, ((0, 0), (0, 128 - depth), (0, 0))).reshape(384, 128)
    sent, s = order((sent, s))
    s = lax.all_gather(s, ("h", "y", "x"), axis=0, tiled=False)
    got = lax.all_gather(sent, Z, axis=0, tiled=False)
    copies = assemble(core, got, width, 2 * per, full)
    at = (feats - (full - 128) + 2 * per * (expert // per) + expert % per).reshape(1)

    w_gate, w_up, w_down = routed_gate[0], routed_up[0], routed_down[0]
    w_in = jnp.concatenate([w_gate, swap(w_gate), w_up, swap(w_up)], 1)
    w_in = jnp.pad(w_in, ((0, full - feats), (0, 0)))
    w_out = jnp.concatenate([w_down, swap(w_down)], 0)
    w_out = jnp.pad(w_out, ((0, 0), (0, full - feats)))

    apply = lambda *blocks: ffn(at, blocks, w_in, w_out)
    held = lax.dynamic_slice_in_dim(copies, lax.axis_index("h") * half, half, 0)
    near, held = order((spread(copies), jnp.concatenate([held, swap(held)], 0)))
    lo, hi = near[: 2 * toks], near[2 * toks :]
    prev_lo, succ_hi = move(lo, 1, 1), move(hi, 1, -1)
    far_lo, far_hi = move(prev_lo, 1, 1), move(succ_hi, 1, -1)
    prev_lo, succ_hi = apply(prev_lo, succ_hi)
    lo, hi, prev_lo, succ_hi = order((lo, hi, prev_lo, succ_hi))
    prev_hi, succ_lo = move(hi, 1, 1), move(lo, 1, -1)
    back_p, back_s = move(prev_lo, 1, -1), move(succ_hi, 1, 1)
    far_lo, far_hi = apply(far_lo, far_hi)

    far_lo, far_hi, prev_hi, succ_lo = order((far_lo, far_hi, prev_hi, succ_lo))
    from_prev, from_succ = move(far_lo, 1, 1), move(far_hi, 1, -1)
    prev_hi, succ_lo = apply(prev_hi, succ_lo)
    prev_hi, succ_lo, s = order((prev_hi, succ_lo, s))
    out = shared_expert(held, s, depth)
    prev_hi, succ_lo = add(prev_hi, from_succ), add(succ_lo, from_prev)
    prev_hi, succ_lo, lo, hi, out, back_p, back_s = order(
        (prev_hi, succ_lo, lo, hi, out, back_p, back_s)
    )
    prev_hi, succ_lo = move(prev_hi, 1, -1), move(succ_lo, 1, 1)
    own_lo, own_hi = apply(lo, hi)
    out = out[:half] + swap(out[half:].astype(bf16)).astype(f32)
    here = jnp.arange(H * half, dtype=jnp.int32)[:, None] // half == lax.axis_index("h")
    shared = jnp.where(here, jnp.concatenate([out] * H, 0), 0.0)
    total = jnp.concatenate([add(own_lo, back_p, succ_lo), add(own_hi, back_s, prev_hi)], 0)
    total = spread(total)
    total = [total[i * toks : (i + 1) * toks] for i in range(4)]
    total = add(shared, *[t[:, :feats] for t in total])

    back = total.reshape(H, half, L, C, width).transpose(0, 2, 3, 1, 4)
    back = jnp.where(core == 0, back, back[:, :, ::-1])
    back = back.reshape(H * L, C * half, width)
    back = lax.all_to_all(back, Z, split_axis=0, concat_axis=0, tiled=True)
    done = jnp.sum(back.astype(f32), axis=0).astype(bf16)
    keep, take = done[:half], swap(done[half:])
    return jnp.where(
        core == 0, jnp.concatenate([keep, take], 0), jnp.concatenate([take, keep], 0)
    )


def solution(mesh):
    fine = Mesh(mesh.devices.reshape(Y, H, X, L, C), AXES)
    in_specs = (
        P(EXPERT, TENSOR),
        P(EXPERT, None),
        P(EXPERT, None),
        P(EXPERT, None, TENSOR),
        P(EXPERT, None, TENSOR),
        P(EXPERT, TENSOR, None),
        P(EXPERT, TENSOR),
        P(EXPERT, TENSOR),
        P(TENSOR, EXPERT),
    )
    return jax.shard_map(
        local, mesh=fine, in_specs=in_specs, out_specs=P(EXPERT, TENSOR), check_vma=False
    )
```

```python
import functools

import jax
import jax.numpy as jnp
from jax import lax
from jax.experimental import pallas as pl
from jax.experimental.pallas import tpu as pltpu
from jax.sharding import Mesh, PartitionSpec as P

Y, H, X, L, C = 4, 2, 4, 8, 2
AXES = ("y", "h", "x", "l", "c")
EXPERT = ("y", "h", "x")
TENSOR = ("l", "c")
Z = ("h", "l")
f32 = jnp.float32
bf16 = jnp.bfloat16


def move(a, stage, k):
    pairs = []
    for y in range(Y):
        for x in range(X):
            for c in range(C):
                to = ((y + k) % Y, x) if (stage + c) % 2 == 0 else (y, (x + k) % X)
                pairs.append(((y * X + x) * C + c, (to[0] * X + to[1]) * C + c))
    return lax.ppermute(a, ("y", "x", "c"), pairs)


def swap(a):
    return lax.ppermute(a, "c", [(0, 1), (1, 0)])


def spread(a):
    groups = [[(y * X + x) * C for y in range(Y)] for x in range(X)]
    groups += [[(y * X + x) * C + 1 for x in range(X)] for y in range(Y)]
    return lax.all_to_all(
        a, ("y", "x", "c"), 0, 0, axis_index_groups=groups, tiled=True
    )


def turn(a):
    return lax.ppermute(a, ("h", "c"), [(h * 2 + c, c * 2 + h) for h in range(2) for c in range(2)])


def add(*terms):
    total = terms[0].astype(f32)
    for t in terms[1:]:
        total = total + t.astype(f32)
    return total.astype(bf16)


def ffn_kernel(at_ref, *refs, hid, parts):
    w_ref, d_ref = refs[parts : parts + 2]
    o_refs = refs[parts + 2 :]
    x = jnp.concatenate([r[...] for r in refs[:parts]], 0)
    width = x.shape[1]
    tail = x[:, width - 128 :].astype(f32)
    lane = lax.broadcasted_iota(jnp.int32, tail.shape, 1)
    at = at_ref[0]
    weight = jnp.sum(
        jnp.where((lane == at) | (lane == at + 2), tail, 0.0), axis=1, keepdims=True
    )
    acts = jnp.dot(x, w_ref[...], preferred_element_type=f32)
    gate, up = acts[:, :hid], acts[:, hid:]
    hidden = (gate / (1.0 + jnp.exp(-gate)) * up * weight).astype(bf16)
    rows = x.shape[0] // parts
    for lo in range(0, width, 512):
        hi = min(lo + 512, width)
        out = jnp.dot(hidden, d_ref[:, lo:hi], preferred_element_type=f32).astype(bf16)
        for i, o_ref in enumerate(o_refs):
            o_ref[:, lo:hi] = out[i * rows : (i + 1) * rows]


def ffn(at, xs, w_in, w_out):
    parts = len(xs)
    rows, width = xs[0].shape
    hid = w_in.shape[1] // 2
    whole = pl.BlockSpec(memory_space=pltpu.VMEM)
    return pl.pallas_call(
        functools.partial(ffn_kernel, hid=hid, parts=parts),
        out_shape=[jax.ShapeDtypeStruct((rows, width), bf16)] * parts,
        in_specs=[pl.BlockSpec(memory_space=pltpu.SMEM)] + [whole] * (parts + 2),
        out_specs=[whole] * parts,
        compiler_params=pltpu.CompilerParams(vmem_limit_bytes=40 * 1024 * 1024),
        cost_estimate=pl.CostEstimate(
            flops=2 * parts * rows * width * 3 * hid,
            bytes_accessed=2 * (2 * parts * rows * width + 3 * width * hid),
            transcendentals=parts * rows * hid,
        ),
    )(at, *xs, w_in, w_out)


def rows_kernel(core_ref, got_ref, o_ref, *, width, extra):
    core = core_ref[0]
    half = got_ref.shape[1]
    for h in range(H):
        own, other, pieces = [], [], []
        for block in range(L):
            v = got_ref[h * L + block]
            own.append(v[:, :256].astype(f32))
            other.append(v[:, 256:].astype(f32))
        for block in range(L):
            pieces.append(jnp.where(core == 0, own[block], other[block]))
            pieces.append(jnp.where(core == 0, other[block], own[block]))
        feats = width * len(pieces)
        used = feats + extra * len(pieces)
        row = jnp.concatenate(
            [p[:, :width] for p in pieces]
            + [p[:, width : width + extra] for p in pieces]
            + [jnp.zeros((half, o_ref.shape[1] - used), f32)],
            1,
        ).astype(bf16)
        for copy in range(o_ref.shape[0] // (H * half)):
            at = (copy * H + h) * half
            o_ref[at : at + half, :] = row


def assemble(core, got, width, extra, full):
    return pl.pallas_call(
        functools.partial(rows_kernel, width=width, extra=extra),
        out_shape=jax.ShapeDtypeStruct((4 * H * got.shape[1], full), bf16),
        in_specs=[
            pl.BlockSpec(memory_space=pltpu.SMEM),
            pl.BlockSpec(memory_space=pltpu.VMEM),
        ],
        out_specs=pl.BlockSpec(memory_space=pltpu.VMEM),
        compiler_params=pltpu.CompilerParams(vmem_limit_bytes=32 * 1024 * 1024),
        cost_estimate=pl.CostEstimate(flops=0, bytes_accessed=3_000_000, transcendentals=0),
    )(core.reshape(1), got)


def shared_kernel(x_ref, s_ref, o_ref, *, depth):
    count = s_ref.shape[0]
    gate = jnp.zeros((x_ref.shape[0], 128), f32)
    up = gate
    for e in range(count):
        x = x_ref[:, e * depth : e * depth + 128]
        gate += jnp.dot(x, s_ref[e, :128, :], preferred_element_type=f32)
        up += jnp.dot(x, s_ref[e, 128:256, :], preferred_element_type=f32)
    hidden = (gate / (1.0 + jnp.exp(-gate)) * up).astype(bf16)
    outs = []
    for e in range(count):
        out = lax.dot_general(
            hidden, s_ref[e, 256:384, :], (((1,), (1,)), ((), ())), preferred_element_type=f32
        )
        outs.append(out[:, :depth])
    o_ref[...] = jnp.concatenate(outs, 1)


def shared_expert(x, s, depth):
    rows, count = x.shape[0], s.shape[0]
    whole = pl.BlockSpec(memory_space=pltpu.VMEM)
    return pl.pallas_call(
        functools.partial(shared_kernel, depth=depth),
        out_shape=jax.ShapeDtypeStruct((rows, count * depth), f32),
        in_specs=[whole] * 2,
        out_specs=whole,
        compiler_params=pltpu.CompilerParams(vmem_limit_bytes=32 * 1024 * 1024),
        cost_estimate=pl.CostEstimate(
            flops=6 * rows * count * 128 * 128, bytes_accessed=6_000_000, transcendentals=rows * 128
        ),
    )(x, s)


def local(
    tokens,
    gate_codes,
    routes,
    routed_gate,
    routed_up,
    routed_down,
    shared_gate,
    shared_up,
    shared_down,
):
    expert = lax.axis_index(EXPERT)
    part = lax.axis_index(TENSOR)
    core = lax.axis_index("c")
    order = lax.optimization_barrier
    toks, width = tokens.shape
    feats = width * L * C
    full = -(-feats // 128) * 128
    n_exp = Y * H * X
    per = n_exp // (L * C)

    gates = gate_codes.astype(f32)
    gates = 2.5 * gates / jnp.sum(gates, axis=1, keepdims=True)
    own = part * per + jnp.arange(per, dtype=jnp.int32)
    table = jnp.sum(jnp.where(routes[:, :, None] == own, gates[:, :, None], 0.0), axis=1)
    high = table.astype(bf16)
    low = (table - high.astype(f32)).astype(bf16)
    sent = jnp.concatenate([high, low, jnp.zeros((toks, 256 - width - 2 * per), bf16)], 1)
    sent = jnp.concatenate([tokens, sent], 1)
    half = toks // C
    sent = jnp.concatenate(
        [
            lax.dynamic_slice_in_dim(sent, core * half, half, 0),
            swap(lax.dynamic_slice_in_dim(sent, (1 - core) * half, half, 0)),
        ],
        1,
    )
    s = jnp.stack([shared_gate, shared_up, shared_down.T])
    depth = s.shape[1]
    s = jnp.pad(s, ((0, 0), (0, 128 - depth), (0, 0))).reshape(384, 128)
    got = lax.all_gather(sent, Z, axis=0, tiled=False)
    got, s = order((got, s))
    s = turn(s)
    copies = assemble(core, got, width, 2 * per, full)
    at = (feats - (full - 128) + 2 * per * (expert // per) + expert % per).reshape(1)

    w_gate, w_up, w_down = routed_gate[0], routed_up[0], routed_down[0]
    w_in = jnp.concatenate([w_gate, swap(w_gate), w_up, swap(w_up)], 1)
    w_in = jnp.pad(w_in, ((0, full - feats), (0, 0)))
    w_out = jnp.concatenate([w_down, swap(w_down)], 0)
    w_out = jnp.pad(w_out, ((0, 0), (0, full - feats)))

    apply = lambda *blocks: ffn(at, blocks, w_in, w_out)
    near, s = order((spread(copies), s))
    s = lax.all_gather(s, ("y", "c", "x"), axis=0, tiled=False)
    lo, hi = near[: 2 * toks], near[2 * toks :]
    prev_lo, succ_hi = move(lo, 1, 1), move(hi, 1, -1)
    far_lo, far_hi = move(prev_lo, 1, 1), move(succ_hi, 1, -1)
    prev_lo, succ_hi = apply(prev_lo, succ_hi)
    lo, hi, prev_lo, succ_hi = order((lo, hi, prev_lo, succ_hi))
    prev_hi, succ_lo = move(hi, 1, 1), move(lo, 1, -1)
    back_p, back_s = move(prev_lo, 1, -1), move(succ_hi, 1, 1)
    far_lo, far_hi = apply(far_lo, far_hi)

    far_lo, far_hi, prev_hi, succ_lo = order((far_lo, far_hi, prev_hi, succ_lo))
    from_prev, from_succ = move(far_lo, 1, 1), move(far_hi, 1, -1)
    prev_hi, succ_lo = apply(prev_hi, succ_lo)
    prev_hi, succ_lo, s = order((prev_hi, succ_lo, s))
    out = shared_expert(copies[:toks], s, depth)
    prev_hi, succ_lo = add(prev_hi, from_succ), add(succ_lo, from_prev)
    prev_hi, succ_lo, lo, hi, out, back_p, back_s = order(
        (prev_hi, succ_lo, lo, hi, out, back_p, back_s)
    )
    prev_hi, succ_lo = move(prev_hi, 1, -1), move(succ_lo, 1, 1)
    own_lo, own_hi = apply(lo, hi)
    total = jnp.concatenate([add(own_lo, back_p, succ_lo), add(own_hi, back_s, prev_hi)], 0)
    total = spread(total)
    total = [total[i * toks : (i + 1) * toks] for i in range(4)]
    total = add(out, *[t[:, :feats] for t in total])

    back = total.reshape(H, half, L, C, width).transpose(0, 2, 3, 1, 4)
    back = jnp.where(core == 0, back, back[:, :, ::-1])
    back = back.reshape(H * L, C * half, width)
    back = lax.all_to_all(back, Z, split_axis=0, concat_axis=0, tiled=True)
    done = jnp.sum(back.astype(f32), axis=0).astype(bf16)
    keep, take = done[:half], swap(done[half:])
    return jnp.where(
        core == 0, jnp.concatenate([keep, take], 0), jnp.concatenate([take, keep], 0)
    )


def solution(mesh):
    fine = Mesh(mesh.devices.reshape(Y, H, X, L, C), AXES)
    in_specs = (
        P(EXPERT, TENSOR),
        P(EXPERT, None),
        P(EXPERT, None),
        P(EXPERT, None, TENSOR),
        P(EXPERT, None, TENSOR),
        P(EXPERT, TENSOR, None),
        P(EXPERT, TENSOR),
        P(EXPERT, TENSOR),
        P(TENSOR, EXPERT),
    )
    return jax.shard_map(
        local, mesh=fine, in_specs=in_specs, out_specs=P(EXPERT, TENSOR), check_vma=False
    )
```

```python
import functools

import jax
import jax.numpy as jnp
from jax import lax
from jax.experimental import pallas as pl
from jax.experimental.pallas import tpu as pltpu
from jax.sharding import Mesh, PartitionSpec as P

Y, H, X, L, C = 4, 2, 4, 8, 2
AXES = ("y", "h", "x", "l", "c")
EXPERT = ("y", "h", "x")
TENSOR = ("l", "c")
Z = ("h", "l")
f32 = jnp.float32
bf16 = jnp.bfloat16


def move(a, stage, k):
    pairs = []
    for y in range(Y):
        for x in range(X):
            for c in range(C):
                to = ((y + k) % Y, x) if (stage + c) % 2 == 0 else (y, (x + k) % X)
                pairs.append(((y * X + x) * C + c, (to[0] * X + to[1]) * C + c))
    return lax.ppermute(a, ("y", "x", "c"), pairs)


def swap(a):
    return lax.ppermute(a, "c", [(0, 1), (1, 0)])


def spread(a):
    groups = [[(y * X + x) * C for y in range(Y)] for x in range(X)]
    groups += [[(y * X + x) * C + 1 for x in range(X)] for y in range(Y)]
    return lax.all_to_all(
        a, ("y", "x", "c"), 0, 0, axis_index_groups=groups, tiled=True
    )


def turn(a):
    return lax.ppermute(a, ("h", "c"), [(h * 2 + c, c * 2 + h) for h in range(2) for c in range(2)])


def add(*terms):
    total = terms[0].astype(f32)
    for t in terms[1:]:
        total = total + t.astype(f32)
    return total.astype(bf16)


def ffn_kernel(at_ref, *refs, hid, parts):
    w_ref, d_ref = refs[parts : parts + 2]
    o_refs = refs[parts + 2 :]
    x = jnp.concatenate([r[...] for r in refs[:parts]], 0)
    width = x.shape[1]
    tail = x[:, width - 128 :].astype(f32)
    lane = lax.broadcasted_iota(jnp.int32, tail.shape, 1)
    at = at_ref[0]
    weight = jnp.sum(
        jnp.where((lane == at) | (lane == at + 2), tail, 0.0), axis=1, keepdims=True
    )
    acts = jnp.dot(x, w_ref[...], preferred_element_type=f32)
    gate, up = acts[:, :hid], acts[:, hid:]
    hidden = (gate / (1.0 + jnp.exp(-gate)) * up * weight).astype(bf16)
    rows = x.shape[0] // parts
    for lo in range(0, width, 512):
        hi = min(lo + 512, width)
        out = jnp.dot(hidden, d_ref[:, lo:hi], preferred_element_type=f32).astype(bf16)
        for i, o_ref in enumerate(o_refs):
            o_ref[:, lo:hi] = out[i * rows : (i + 1) * rows]


def ffn(at, xs, w_in, w_out):
    parts = len(xs)
    rows, width = xs[0].shape
    hid = w_in.shape[1] // 2
    whole = pl.BlockSpec(memory_space=pltpu.VMEM)
    return pl.pallas_call(
        functools.partial(ffn_kernel, hid=hid, parts=parts),
        out_shape=[jax.ShapeDtypeStruct((rows, width), bf16)] * parts,
        in_specs=[pl.BlockSpec(memory_space=pltpu.SMEM)] + [whole] * (parts + 2),
        out_specs=[whole] * parts,
        compiler_params=pltpu.CompilerParams(vmem_limit_bytes=40 * 1024 * 1024),
        cost_estimate=pl.CostEstimate(
            flops=2 * parts * rows * width * 3 * hid,
            bytes_accessed=2 * (2 * parts * rows * width + 3 * width * hid),
            transcendentals=parts * rows * hid,
        ),
    )(at, *xs, w_in, w_out)


def rows_kernel(core_ref, got_ref, o_ref, *, width, extra):
    core = core_ref[0]
    half = got_ref.shape[1]
    for h in range(H):
        own, other, pieces = [], [], []
        for block in range(L):
            v = got_ref[h * L + block]
            own.append(v[:, :256].astype(f32))
            other.append(v[:, 256:].astype(f32))
        for block in range(L):
            pieces.append(jnp.where(core == 0, own[block], other[block]))
            pieces.append(jnp.where(core == 0, other[block], own[block]))
        feats = width * len(pieces)
        used = feats + extra * len(pieces)
        row = jnp.concatenate(
            [p[:, :width] for p in pieces]
            + [p[:, width : width + extra] for p in pieces]
            + [jnp.zeros((half, o_ref.shape[1] - used), f32)],
            1,
        ).astype(bf16)
        for copy in range(o_ref.shape[0] // (H * half)):
            at = (copy * H + h) * half
            o_ref[at : at + half, :] = row


def assemble(core, got, width, extra, full):
    return pl.pallas_call(
        functools.partial(rows_kernel, width=width, extra=extra),
        out_shape=jax.ShapeDtypeStruct((4 * H * got.shape[1], full), bf16),
        in_specs=[
            pl.BlockSpec(memory_space=pltpu.SMEM),
            pl.BlockSpec(memory_space=pltpu.VMEM),
        ],
        out_specs=pl.BlockSpec(memory_space=pltpu.VMEM),
        compiler_params=pltpu.CompilerParams(vmem_limit_bytes=32 * 1024 * 1024),
        cost_estimate=pl.CostEstimate(flops=0, bytes_accessed=3_000_000, transcendentals=0),
    )(core.reshape(1), got)


def shared_kernel(x_ref, s_ref, o_ref, *, depth):
    count = s_ref.shape[0]
    gate = jnp.zeros((x_ref.shape[0], 128), f32)
    up = gate
    for e in range(count):
        x = x_ref[:, e * depth : e * depth + 128]
        gate += jnp.dot(x, s_ref[e, :128, :], preferred_element_type=f32)
        up += jnp.dot(x, s_ref[e, 128:256, :], preferred_element_type=f32)
    hidden = (gate / (1.0 + jnp.exp(-gate)) * up).astype(bf16)
    outs = []
    for e in range(count):
        out = lax.dot_general(
            hidden, s_ref[e, 256:384, :], (((1,), (1,)), ((), ())), preferred_element_type=f32
        )
        outs.append(out[:, :depth])
    o_ref[...] = jnp.concatenate(outs, 1)


def shared_expert(x, s, depth):
    rows, count = x.shape[0], s.shape[0]
    whole = pl.BlockSpec(memory_space=pltpu.VMEM)
    return pl.pallas_call(
        functools.partial(shared_kernel, depth=depth),
        out_shape=jax.ShapeDtypeStruct((rows, count * depth), f32),
        in_specs=[whole] * 2,
        out_specs=whole,
        compiler_params=pltpu.CompilerParams(vmem_limit_bytes=32 * 1024 * 1024),
        cost_estimate=pl.CostEstimate(
            flops=6 * rows * count * 128 * 128, bytes_accessed=6_000_000, transcendentals=rows * 128
        ),
    )(x, s)


def local(
    tokens,
    gate_codes,
    routes,
    routed_gate,
    routed_up,
    routed_down,
    shared_gate,
    shared_up,
    shared_down,
):
    expert = lax.axis_index(EXPERT)
    part = lax.axis_index(TENSOR)
    core = lax.axis_index("c")
    order = lax.optimization_barrier
    toks, width = tokens.shape
    feats = width * L * C
    full = -(-feats // 128) * 128
    n_exp = Y * H * X
    per = n_exp // (L * C)

    gates = gate_codes.astype(f32)
    gates = 2.5 * gates / jnp.sum(gates, axis=1, keepdims=True)
    own = part * per + jnp.arange(per, dtype=jnp.int32)
    table = jnp.sum(jnp.where(routes[:, :, None] == own, gates[:, :, None], 0.0), axis=1)
    high = table.astype(bf16)
    low = (table - high.astype(f32)).astype(bf16)
    sent = jnp.concatenate([high, low, jnp.zeros((toks, 256 - width - 2 * per), bf16)], 1)
    sent = jnp.concatenate([tokens, sent], 1)
    half = toks // C
    sent = jnp.concatenate(
        [
            lax.dynamic_slice_in_dim(sent, core * half, half, 0),
            swap(lax.dynamic_slice_in_dim(sent, (1 - core) * half, half, 0)),
        ],
        1,
    )
    s = jnp.stack([shared_gate, shared_up, shared_down.T])
    depth = s.shape[1]
    s = jnp.pad(s, ((0, 0), (0, 128 - depth), (0, 0))).reshape(384, 128)
    got = lax.all_gather(sent, Z, axis=0, tiled=False)
    copies, s = order((assemble(core, got, width, 2 * per, full), turn(s)))
    s = lax.all_gather(s, ("y", "c", "x"), axis=0, tiled=False)
    at = (feats - (full - 128) + 2 * per * (expert // per) + expert % per).reshape(1)

    w_gate, w_up, w_down = routed_gate[0], routed_up[0], routed_down[0]
    w_in = jnp.concatenate([w_gate, swap(w_gate), w_up, swap(w_up)], 1)
    w_in = jnp.pad(w_in, ((0, full - feats), (0, 0)))
    w_out = jnp.concatenate([w_down, swap(w_down)], 0)
    w_out = jnp.pad(w_out, ((0, 0), (0, full - feats)))

    apply = lambda *blocks: ffn(at, blocks, w_in, w_out)
    near = spread(copies)
    lo, hi = near[: 2 * toks], near[2 * toks :]
    prev_lo, succ_hi = move(lo, 1, 1), move(hi, 1, -1)
    far_lo, far_hi = move(prev_lo, 1, 1), move(succ_hi, 1, -1)
    prev_lo, succ_hi = apply(prev_lo, succ_hi)
    lo, hi, prev_lo, succ_hi = order((lo, hi, prev_lo, succ_hi))
    prev_hi, succ_lo = move(hi, 1, 1), move(lo, 1, -1)
    back_p, back_s = move(prev_lo, 1, -1), move(succ_hi, 1, 1)
    far_lo, far_hi = apply(far_lo, far_hi)

    far_lo, far_hi, prev_hi, succ_lo = order((far_lo, far_hi, prev_hi, succ_lo))
    from_prev, from_succ = move(far_lo, 1, 1), move(far_hi, 1, -1)
    prev_hi, succ_lo = apply(prev_hi, succ_lo)
    prev_hi, succ_lo, s = order((prev_hi, succ_lo, s))
    out = shared_expert(copies[:toks], s, depth)
    prev_hi, succ_lo = add(prev_hi, from_succ), add(succ_lo, from_prev)
    prev_hi, succ_lo, lo, hi, out, back_p, back_s = order(
        (prev_hi, succ_lo, lo, hi, out, back_p, back_s)
    )
    prev_hi, succ_lo = move(prev_hi, 1, -1), move(succ_lo, 1, 1)
    own_lo, own_hi = apply(lo, hi)
    total = jnp.concatenate([add(own_lo, back_p, succ_lo), add(own_hi, back_s, prev_hi)], 0)
    total = spread(total)
    total = [total[i * toks : (i + 1) * toks] for i in range(4)]
    total = add(out, *[t[:, :feats] for t in total])

    back = total.reshape(H, half, L, C, width).transpose(0, 2, 3, 1, 4)
    back = jnp.where(core == 0, back, back[:, :, ::-1])
    back = back.reshape(H * L, C * half, width)
    back = lax.all_to_all(back, Z, split_axis=0, concat_axis=0, tiled=True)
    done = jnp.sum(back.astype(f32), axis=0).astype(bf16)
    keep, take = done[:half], swap(done[half:])
    return jnp.where(
        core == 0, jnp.concatenate([keep, take], 0), jnp.concatenate([take, keep], 0)
    )


def solution(mesh):
    fine = Mesh(mesh.devices.reshape(Y, H, X, L, C), AXES)
    in_specs = (
        P(EXPERT, TENSOR),
        P(EXPERT, None),
        P(EXPERT, None),
        P(EXPERT, None, TENSOR),
        P(EXPERT, None, TENSOR),
        P(EXPERT, TENSOR, None),
        P(EXPERT, TENSOR),
        P(EXPERT, TENSOR),
        P(TENSOR, EXPERT),
    )
    return jax.shard_map(
        local, mesh=fine, in_specs=in_specs, out_specs=P(EXPERT, TENSOR), check_vma=False
    )
```

```python
import functools

import jax
import jax.numpy as jnp
from jax import lax
from jax.experimental import pallas as pl
from jax.experimental.pallas import tpu as pltpu
from jax.sharding import Mesh, PartitionSpec as P

Y, H, X, L, C = 4, 2, 4, 8, 2
AXES = ("y", "h", "x", "l", "c")
EXPERT = ("y", "h", "x")
TENSOR = ("l", "c")
Z = ("h", "l")
f32 = jnp.float32
bf16 = jnp.bfloat16


def move(a, stage, k):
    pairs = []
    for y in range(Y):
        for x in range(X):
            for c in range(C):
                to = ((y + k) % Y, x) if (stage + c) % 2 == 0 else (y, (x + k) % X)
                pairs.append(((y * X + x) * C + c, (to[0] * X + to[1]) * C + c))
    return lax.ppermute(a, ("y", "x", "c"), pairs)


def swap(a):
    return lax.ppermute(a, "c", [(0, 1), (1, 0)])


def spread(a):
    groups = [[(y * X + x) * C for y in range(Y)] for x in range(X)]
    groups += [[(y * X + x) * C + 1 for x in range(X)] for y in range(Y)]
    return lax.all_to_all(
        a, ("y", "x", "c"), 0, 0, axis_index_groups=groups, tiled=True
    )


def turn(a):
    return lax.ppermute(a, ("h", "c"), [(h * 2 + c, c * 2 + h) for h in range(2) for c in range(2)])


def add(*terms):
    total = terms[0].astype(f32)
    for t in terms[1:]:
        total = total + t.astype(f32)
    return total.astype(bf16)


def ffn_kernel(at_ref, *refs, hid, parts):
    w_ref, d_ref = refs[parts : parts + 2]
    o_refs = refs[parts + 2 :]
    x = jnp.concatenate([r[...] for r in refs[:parts]], 0)
    width = x.shape[1]
    tail = x[:, width - 128 :].astype(f32)
    lane = lax.broadcasted_iota(jnp.int32, tail.shape, 1)
    at = at_ref[0]
    weight = jnp.sum(
        jnp.where((lane == at) | (lane == at + 2), tail, 0.0), axis=1, keepdims=True
    )
    acts = jnp.dot(x, w_ref[...], preferred_element_type=f32)
    gate, up = acts[:, :hid], acts[:, hid:]
    hidden = (gate / (1.0 + jnp.exp(-gate)) * up * weight).astype(bf16)
    rows = x.shape[0] // parts
    for lo in range(0, width, 512):
        hi = min(lo + 512, width)
        out = jnp.dot(hidden, d_ref[:, lo:hi], preferred_element_type=f32).astype(bf16)
        for i, o_ref in enumerate(o_refs):
            o_ref[:, lo:hi] = out[i * rows : (i + 1) * rows]


def ffn(at, xs, w_in, w_out):
    parts = len(xs)
    rows, width = xs[0].shape
    hid = w_in.shape[1] // 2
    whole = pl.BlockSpec(memory_space=pltpu.VMEM)
    return pl.pallas_call(
        functools.partial(ffn_kernel, hid=hid, parts=parts),
        out_shape=[jax.ShapeDtypeStruct((rows, width), bf16)] * parts,
        in_specs=[pl.BlockSpec(memory_space=pltpu.SMEM)] + [whole] * (parts + 2),
        out_specs=[whole] * parts,
        compiler_params=pltpu.CompilerParams(vmem_limit_bytes=40 * 1024 * 1024),
        cost_estimate=pl.CostEstimate(
            flops=2 * parts * rows * width * 3 * hid,
            bytes_accessed=2 * (2 * parts * rows * width + 3 * width * hid),
            transcendentals=parts * rows * hid,
        ),
    )(at, *xs, w_in, w_out)


def rows_kernel(core_ref, got_ref, o_ref, *, width, extra):
    core = core_ref[0]
    half = got_ref.shape[1]
    for h in range(H):
        own, other, pieces = [], [], []
        for block in range(L):
            v = got_ref[h * L + block]
            own.append(v[:, :256].astype(f32))
            other.append(v[:, 256:].astype(f32))
        for block in range(L):
            pieces.append(jnp.where(core == 0, own[block], other[block]))
            pieces.append(jnp.where(core == 0, other[block], own[block]))
        feats = width * len(pieces)
        used = feats + extra * len(pieces)
        row = jnp.concatenate(
            [p[:, :width] for p in pieces]
            + [p[:, width : width + extra] for p in pieces]
            + [jnp.zeros((half, o_ref.shape[1] - used), f32)],
            1,
        ).astype(bf16)
        for copy in range(o_ref.shape[0] // (H * half)):
            at = (copy * H + h) * half
            o_ref[at : at + half, :] = row


def assemble(core, got, width, extra, full):
    return pl.pallas_call(
        functools.partial(rows_kernel, width=width, extra=extra),
        out_shape=jax.ShapeDtypeStruct((4 * H * got.shape[1], full), bf16),
        in_specs=[
            pl.BlockSpec(memory_space=pltpu.SMEM),
            pl.BlockSpec(memory_space=pltpu.VMEM),
        ],
        out_specs=pl.BlockSpec(memory_space=pltpu.VMEM),
        compiler_params=pltpu.CompilerParams(vmem_limit_bytes=32 * 1024 * 1024),
        cost_estimate=pl.CostEstimate(flops=0, bytes_accessed=3_000_000, transcendentals=0),
    )(core.reshape(1), got)


def shared_kernel(x_ref, s_ref, o_ref, *, depth):
    count = s_ref.shape[0]
    gate = jnp.zeros((x_ref.shape[0], 128), f32)
    up = gate
    for e in range(count):
        x = x_ref[:, e * depth : e * depth + 128]
        gate += jnp.dot(x, s_ref[e, :128, :], preferred_element_type=f32)
        up += jnp.dot(x, s_ref[e, 128:256, :], preferred_element_type=f32)
    hidden = (gate / (1.0 + jnp.exp(-gate)) * up).astype(bf16)
    outs = []
    for e in range(count):
        out = lax.dot_general(
            hidden, s_ref[e, 256:384, :], (((1,), (1,)), ((), ())), preferred_element_type=f32
        )
        outs.append(out[:, :depth])
    o_ref[...] = jnp.concatenate(outs, 1)


def shared_expert(x, s, depth):
    rows, count = x.shape[0], s.shape[0]
    whole = pl.BlockSpec(memory_space=pltpu.VMEM)
    return pl.pallas_call(
        functools.partial(shared_kernel, depth=depth),
        out_shape=jax.ShapeDtypeStruct((rows, count * depth), f32),
        in_specs=[whole] * 2,
        out_specs=whole,
        compiler_params=pltpu.CompilerParams(vmem_limit_bytes=32 * 1024 * 1024),
        cost_estimate=pl.CostEstimate(
            flops=6 * rows * count * 128 * 128, bytes_accessed=6_000_000, transcendentals=rows * 128
        ),
    )(x, s)


def local(
    tokens,
    gate_codes,
    routes,
    routed_gate,
    routed_up,
    routed_down,
    shared_gate,
    shared_up,
    shared_down,
):
    expert = lax.axis_index(EXPERT)
    part = lax.axis_index(TENSOR)
    core = lax.axis_index("c")
    order = lax.optimization_barrier
    toks, width = tokens.shape
    feats = width * L * C
    full = -(-feats // 128) * 128
    n_exp = Y * H * X
    per = n_exp // (L * C)

    gates = gate_codes.astype(f32)
    gates = 2.5 * gates / jnp.sum(gates, axis=1, keepdims=True)
    own = part * per + jnp.arange(per, dtype=jnp.int32)
    table = jnp.sum(jnp.where(routes[:, :, None] == own, gates[:, :, None], 0.0), axis=1)
    high = table.astype(bf16)
    low = (table - high.astype(f32)).astype(bf16)
    sent = jnp.concatenate([high, low, jnp.zeros((toks, 256 - width - 2 * per), bf16)], 1)
    sent = jnp.concatenate([tokens, sent], 1)
    half = toks // C
    sent = jnp.concatenate(
        [
            lax.dynamic_slice_in_dim(sent, core * half, half, 0),
            swap(lax.dynamic_slice_in_dim(sent, (1 - core) * half, half, 0)),
        ],
        1,
    )
    s = jnp.stack([shared_gate, shared_up, shared_down.T])
    depth = s.shape[1]
    s = jnp.pad(s, ((0, 0), (0, 128 - depth), (0, 0))).reshape(384, 128)
    got = lax.all_gather(sent, Z, axis=0, tiled=False)
    copies, s = order((assemble(core, got, width, 2 * per, full), turn(s)))
    s = lax.all_gather(s, ("y", "c", "x"), axis=0, tiled=False)
    at = (feats - (full - 128) + 2 * per * (expert // per) + expert % per).reshape(1)

    w_gate, w_up, w_down = routed_gate[0], routed_up[0], routed_down[0]
    w_in = jnp.concatenate([w_gate, swap(w_gate), w_up, swap(w_up)], 1)
    w_in = jnp.pad(w_in, ((0, full - feats), (0, 0)))
    w_out = jnp.concatenate([w_down, swap(w_down)], 0)
    w_out = jnp.pad(w_out, ((0, 0), (0, full - feats)))

    apply = lambda *blocks: ffn(at, blocks, w_in, w_out)
    near = spread(copies)
    lo, hi = near[: 2 * toks], near[2 * toks :]
    prev_lo, succ_hi = move(lo, 1, 1), move(hi, 1, -1)
    far_lo, far_hi = move(prev_lo, 1, 1), move(succ_hi, 1, -1)
    prev_lo, succ_hi = apply(prev_lo, succ_hi)
    lo, hi, prev_lo, succ_hi = order((lo, hi, prev_lo, succ_hi))
    prev_hi, succ_lo = move(hi, 1, 1), move(lo, 1, -1)
    back_p, back_s = move(prev_lo, 1, -1), move(succ_hi, 1, 1)
    far_lo, far_hi = apply(far_lo, far_hi)

    from_prev, from_succ = move(far_lo, 1, 1), move(far_hi, 1, -1)
    prev_hi, succ_lo, back_p, back_s, _ = order((prev_hi, succ_lo, back_p, back_s, far_lo))
    prev_hi, succ_lo = apply(prev_hi, succ_lo)
    prev_hi, succ_lo, s = order((prev_hi, succ_lo, s))
    out = shared_expert(copies[:toks], s, depth)
    prev_hi, succ_lo = add(prev_hi, from_succ), add(succ_lo, from_prev)
    prev_hi, succ_lo, lo, hi, out = order((prev_hi, succ_lo, lo, hi, out))
    prev_hi, succ_lo = move(prev_hi, 1, -1), move(succ_lo, 1, 1)
    own_lo, own_hi = apply(lo, hi)
    total = jnp.concatenate([add(own_lo, back_p, succ_lo), add(own_hi, back_s, prev_hi)], 0)
    total = spread(total)
    total = [total[i * toks : (i + 1) * toks] for i in range(4)]
    total = add(out, *[t[:, :feats] for t in total])

    back = total.reshape(H, half, L, C, width).transpose(0, 2, 3, 1, 4)
    back = jnp.where(core == 0, back, back[:, :, ::-1])
    back = back.reshape(H * L, C * half, width)
    back = lax.all_to_all(back, Z, split_axis=0, concat_axis=0, tiled=True)
    done = jnp.sum(back.astype(f32), axis=0).astype(bf16)
    keep, take = done[:half], swap(done[half:])
    return jnp.where(
        core == 0, jnp.concatenate([keep, take], 0), jnp.concatenate([take, keep], 0)
    )


def solution(mesh):
    fine = Mesh(mesh.devices.reshape(Y, H, X, L, C), AXES)
    in_specs = (
        P(EXPERT, TENSOR),
        P(EXPERT, None),
        P(EXPERT, None),
        P(EXPERT, None, TENSOR),
        P(EXPERT, None, TENSOR),
        P(EXPERT, TENSOR, None),
        P(EXPERT, TENSOR),
        P(EXPERT, TENSOR),
        P(TENSOR, EXPERT),
    )
    return jax.shard_map(
        local, mesh=fine, in_specs=in_specs, out_specs=P(EXPERT, TENSOR), check_vma=False
    )
```

```python
import functools

import jax
import jax.numpy as jnp
from jax import lax
from jax.experimental import pallas as pl
from jax.experimental.pallas import tpu as pltpu
from jax.sharding import Mesh, PartitionSpec as P

Y, H, X, L, C = 4, 2, 4, 8, 2
AXES = ("y", "h", "x", "l", "c")
EXPERT = ("y", "h", "x")
TENSOR = ("l", "c")
Z = ("h", "l")
f32 = jnp.float32
bf16 = jnp.bfloat16


def move(a, stage, k):
    pairs = []
    for y in range(Y):
        for x in range(X):
            for c in range(C):
                to = ((y + k) % Y, x) if (stage + c) % 2 == 0 else (y, (x + k) % X)
                pairs.append(((y * X + x) * C + c, (to[0] * X + to[1]) * C + c))
    return lax.ppermute(a, ("y", "x", "c"), pairs)


def swap(a):
    return lax.ppermute(a, "c", [(0, 1), (1, 0)])


def spread(a):
    groups = [[(y * X + x) * C for y in range(Y)] for x in range(X)]
    groups += [[(y * X + x) * C + 1 for x in range(X)] for y in range(Y)]
    return lax.all_to_all(
        a, ("y", "x", "c"), 0, 0, axis_index_groups=groups, tiled=True
    )


def turn(a):
    return lax.ppermute(a, ("h", "c"), [(h * 2 + c, c * 2 + h) for h in range(2) for c in range(2)])


def add(*terms):
    total = terms[0].astype(f32)
    for t in terms[1:]:
        total = total + t.astype(f32)
    return total.astype(bf16)


def ffn_kernel(at_ref, *refs, hid, parts):
    w_ref, d_ref = refs[parts : parts + 2]
    o_refs = refs[parts + 2 :]
    x = jnp.concatenate([r[...] for r in refs[:parts]], 0)
    width = x.shape[1]
    tail = x[:, width - 128 :].astype(f32)
    lane = lax.broadcasted_iota(jnp.int32, tail.shape, 1)
    at = at_ref[0]
    weight = jnp.sum(
        jnp.where((lane == at) | (lane == at + 2), tail, 0.0), axis=1, keepdims=True
    )
    acts = jnp.dot(x, w_ref[...], preferred_element_type=f32)
    gate, up = acts[:, :hid], acts[:, hid:]
    hidden = (gate / (1.0 + jnp.exp(-gate)) * up * weight).astype(bf16)
    rows = x.shape[0] // parts
    for lo in range(0, width, 512):
        hi = min(lo + 512, width)
        out = jnp.dot(hidden, d_ref[:, lo:hi], preferred_element_type=f32).astype(bf16)
        for i, o_ref in enumerate(o_refs):
            o_ref[:, lo:hi] = out[i * rows : (i + 1) * rows]


def ffn(at, xs, w_in, w_out):
    parts = len(xs)
    rows, width = xs[0].shape
    hid = w_in.shape[1] // 2
    whole = pl.BlockSpec(memory_space=pltpu.VMEM)
    return pl.pallas_call(
        functools.partial(ffn_kernel, hid=hid, parts=parts),
        out_shape=[jax.ShapeDtypeStruct((rows, width), bf16)] * parts,
        in_specs=[pl.BlockSpec(memory_space=pltpu.SMEM)] + [whole] * (parts + 2),
        out_specs=[whole] * parts,
        compiler_params=pltpu.CompilerParams(vmem_limit_bytes=40 * 1024 * 1024),
        cost_estimate=pl.CostEstimate(
            flops=2 * parts * rows * width * 3 * hid,
            bytes_accessed=2 * (2 * parts * rows * width + 3 * width * hid),
            transcendentals=parts * rows * hid,
        ),
    )(at, *xs, w_in, w_out)


def rows_kernel(core_ref, got_ref, o_ref, *, width, extra):
    core = core_ref[0]
    half = got_ref.shape[1]
    for h in range(H):
        own, other, pieces = [], [], []
        for block in range(L):
            v = got_ref[h * L + block]
            own.append(v[:, :256].astype(f32))
            other.append(v[:, 256:].astype(f32))
        for block in range(L):
            pieces.append(jnp.where(core == 0, own[block], other[block]))
            pieces.append(jnp.where(core == 0, other[block], own[block]))
        feats = width * len(pieces)
        used = feats + extra * len(pieces)
        row = jnp.concatenate(
            [p[:, :width] for p in pieces]
            + [p[:, width : width + extra] for p in pieces]
            + [jnp.zeros((half, o_ref.shape[1] - used), f32)],
            1,
        ).astype(bf16)
        for copy in range(o_ref.shape[0] // (H * half)):
            at = (copy * H + h) * half
            o_ref[at : at + half, :] = row


def assemble(core, got, width, extra, full):
    return pl.pallas_call(
        functools.partial(rows_kernel, width=width, extra=extra),
        out_shape=jax.ShapeDtypeStruct((4 * H * got.shape[1], full), bf16),
        in_specs=[
            pl.BlockSpec(memory_space=pltpu.SMEM),
            pl.BlockSpec(memory_space=pltpu.VMEM),
        ],
        out_specs=pl.BlockSpec(memory_space=pltpu.VMEM),
        compiler_params=pltpu.CompilerParams(vmem_limit_bytes=32 * 1024 * 1024),
        cost_estimate=pl.CostEstimate(flops=0, bytes_accessed=3_000_000, transcendentals=0),
    )(core.reshape(1), got)


def shared_kernel(x_ref, s_ref, o_ref, *, depth):
    count = s_ref.shape[0]
    gate = jnp.zeros((x_ref.shape[0], 128), f32)
    up = gate
    for e in range(count):
        x = x_ref[:, e * depth : e * depth + 128]
        gate += jnp.dot(x, s_ref[e, :128, :], preferred_element_type=f32)
        up += jnp.dot(x, s_ref[e, 128:256, :], preferred_element_type=f32)
    hidden = (gate / (1.0 + jnp.exp(-gate)) * up).astype(bf16)
    outs = []
    for e in range(count):
        out = lax.dot_general(
            hidden, s_ref[e, 256:384, :], (((1,), (1,)), ((), ())), preferred_element_type=f32
        )
        outs.append(out[:, :depth])
    o_ref[...] = jnp.concatenate(outs, 1)


def shared_expert(x, s, depth):
    rows, count = x.shape[0], s.shape[0]
    whole = pl.BlockSpec(memory_space=pltpu.VMEM)
    return pl.pallas_call(
        functools.partial(shared_kernel, depth=depth),
        out_shape=jax.ShapeDtypeStruct((rows, count * depth), f32),
        in_specs=[whole] * 2,
        out_specs=whole,
        compiler_params=pltpu.CompilerParams(vmem_limit_bytes=32 * 1024 * 1024),
        cost_estimate=pl.CostEstimate(
            flops=6 * rows * count * 128 * 128, bytes_accessed=6_000_000, transcendentals=rows * 128
        ),
    )(x, s)


def local(
    tokens,
    gate_codes,
    routes,
    routed_gate,
    routed_up,
    routed_down,
    shared_gate,
    shared_up,
    shared_down,
):
    expert = lax.axis_index(EXPERT)
    part = lax.axis_index(TENSOR)
    core = lax.axis_index("c")
    order = lax.optimization_barrier
    toks, width = tokens.shape
    feats = width * L * C
    full = -(-feats // 128) * 128
    n_exp = Y * H * X
    per = n_exp // (L * C)

    gates = gate_codes.astype(f32)
    gates = 2.5 * gates / jnp.sum(gates, axis=1, keepdims=True)
    own = part * per + jnp.arange(per, dtype=jnp.int32)
    table = jnp.sum(jnp.where(routes[:, :, None] == own, gates[:, :, None], 0.0), axis=1)
    high = table.astype(bf16)
    low = (table - high.astype(f32)).astype(bf16)
    sent = jnp.concatenate([high, low, jnp.zeros((toks, 256 - width - 2 * per), bf16)], 1)
    sent = jnp.concatenate([tokens, sent], 1)
    half = toks // C
    sent = jnp.concatenate(
        [
            lax.dynamic_slice_in_dim(sent, core * half, half, 0),
            swap(lax.dynamic_slice_in_dim(sent, (1 - core) * half, half, 0)),
        ],
        1,
    )
    s = jnp.stack([shared_gate, shared_up, shared_down.T])
    depth = s.shape[1]
    s = jnp.pad(s, ((0, 0), (0, 128 - depth), (0, 0))).reshape(384, 128)
    got = lax.all_gather(sent, Z, axis=0, tiled=False)
    copies, s = order((assemble(core, got, width, 2 * per, full), turn(s)))
    s = lax.all_gather(s, ("y", "c", "x"), axis=0, tiled=False)
    at = (feats - (full - 128) + 2 * per * (expert // per) + expert % per).reshape(1)

    apply = lambda *blocks: ffn(at, blocks, w_in, w_out)
    w_gate, w_up, w_down = routed_gate[0], routed_up[0], routed_down[0]
    near, o_gate, o_up, o_down = order((spread(copies), swap(w_gate), swap(w_up), swap(w_down)))
    w_in = jnp.concatenate([w_gate, o_gate, w_up, o_up], 1)
    w_in = jnp.pad(w_in, ((0, full - feats), (0, 0)))
    w_out = jnp.concatenate([w_down, o_down], 0)
    w_out = jnp.pad(w_out, ((0, 0), (0, full - feats)))
    lo, hi = near[: 2 * toks], near[2 * toks :]
    prev_lo, succ_hi = move(lo, 1, 1), move(hi, 1, -1)
    far_lo, far_hi = move(prev_lo, 1, 1), move(succ_hi, 1, -1)
    prev_lo, succ_hi = apply(prev_lo, succ_hi)
    lo, hi, prev_lo, succ_hi = order((lo, hi, prev_lo, succ_hi))
    prev_hi, succ_lo = move(hi, 1, 1), move(lo, 1, -1)
    back_p, back_s = move(prev_lo, 1, -1), move(succ_hi, 1, 1)
    far_lo, far_hi = apply(far_lo, far_hi)

    from_prev, from_succ = move(far_lo, 1, 1), move(far_hi, 1, -1)
    prev_hi, succ_lo, back_p, back_s, _ = order((prev_hi, succ_lo, back_p, back_s, far_lo))
    prev_hi, succ_lo = apply(prev_hi, succ_lo)
    prev_hi, succ_lo, s = order((prev_hi, succ_lo, s))
    out = shared_expert(copies[:toks], s, depth)
    prev_hi, succ_lo = add(prev_hi, from_succ), add(succ_lo, from_prev)
    prev_hi, succ_lo, lo, hi, out = order((prev_hi, succ_lo, lo, hi, out))
    prev_hi, succ_lo = move(prev_hi, 1, -1), move(succ_lo, 1, 1)
    own_lo, own_hi = apply(lo, hi)
    total = jnp.concatenate([add(own_lo, back_p, succ_lo), add(own_hi, back_s, prev_hi)], 0)
    total = spread(total)
    total = [total[i * toks : (i + 1) * toks] for i in range(4)]
    total = add(out, *[t[:, :feats] for t in total])

    back = total.reshape(H, half, L, C, width).transpose(0, 2, 3, 1, 4)
    back = jnp.where(core == 0, back, back[:, :, ::-1])
    back = back.reshape(H * L, C * half, width)
    back = lax.all_to_all(back, Z, split_axis=0, concat_axis=0, tiled=True)
    done = jnp.sum(back.astype(f32), axis=0).astype(bf16)
    keep, take = done[:half], swap(done[half:])
    return jnp.where(
        core == 0, jnp.concatenate([keep, take], 0), jnp.concatenate([take, keep], 0)
    )


def solution(mesh):
    fine = Mesh(mesh.devices.reshape(Y, H, X, L, C), AXES)
    in_specs = (
        P(EXPERT, TENSOR),
        P(EXPERT, None),
        P(EXPERT, None),
        P(EXPERT, None, TENSOR),
        P(EXPERT, None, TENSOR),
        P(EXPERT, TENSOR, None),
        P(EXPERT, TENSOR),
        P(EXPERT, TENSOR),
        P(TENSOR, EXPERT),
    )
    return jax.shard_map(
        local, mesh=fine, in_specs=in_specs, out_specs=P(EXPERT, TENSOR), check_vma=False
    )
```
